512 devices in a mesh: ctx: 32 (over y, x), exp: 16 (over z, core).
Axes of the slice: x: 4, y: 8, z: 8, core: 2. Of those that a mesh axis runs over, the one named last changes fastest.
Arguments:
- query_proj: bfloat16 [16384, 2048], P('ctx', 'exp'), may hold values from -6 to 6
- key_proj: bfloat16 [16384, 2048], P('ctx', 'exp'), may hold values from -6 to 6
- value_proj: bfloat16 [16384, 4096], P('ctx', 'exp'), may hold values from -6 to 6
- output_gate: bfloat16 [16384, 4096], P('ctx', 'exp'), may hold values from -6 to 6
- beta_logit: float32 [32, 16384], P('exp', 'ctx'), may hold values from -6 to 6
- log_decay: float32 [32, 16384], P('exp', 'ctx'), may hold values from -3 to 0
- norm_gain: float32 [128], replicated, may hold values from 0.1 to 1.9
- out_weight: bfloat16 [4096, 2048], P('exp'), may hold values from -0.09375 to 0.09375
- residual: bfloat16 [16384, 2048], P(('ctx', 'exp')), may hold values from -6 to 6
- moe_gain: float32 [2048], replicated, may hold values from 0.1 to 1.9
- expert_ids: int32 [16384, 10], P(('ctx', 'exp')), may hold values from 0 to 63, all different within a row; in each aligned block of 32 rows (0 to 31, 32 to 63, ...) at most 6 rows name the same one
- route_weight: float32 [16384, 10], P(('ctx', 'exp')), may hold values from 0.02 to 0.2
- expert_gate: bfloat16 [64, 2048, 512], P('ctx', 'exp'), may hold values from -0.125 to 0.125
- expert_up: bfloat16 [64, 2048, 512], P('ctx', 'exp'), may hold values from -0.125 to 0.125
- expert_down: bfloat16 [64, 512, 2048], P('ctx', None, 'exp'), may hold values from -0.25 to 0.25
Outputs:
- layer_out: bfloat16 [16384, 2048], P(('ctx', 'exp'))
The draws below stay inside these ranges and needn't reach their ends.
Inputs may be any that keep to these rules, and one draw needn't show every extreme that they name: `expert_ids`: each row names 10 different experts. Among the 32 rows of one device no expert is named by more than 6 rows, and in some devices one expert is named by exactly 6 of them.
All inputs are finite; a program needn't handle non-finite values.
Results may differ from the reference program's by a relative error of at most 0.018.
Values may be sent and summed in bfloat16 or wider, within the bound.
No kernel may reach another device: no remote copies, remote signals or barrier semaphores. Data moves between devices by JAX's collectives and lax.ppermute only.
A program may use at most 64 MiB of HBM per device.

```python
import math
import jax
import jax.numpy as jnp
import numpy as np
from jax import lax

D = 2048
DK = 128
DV = 128
FH = 512
TOPK = 10
HV_DEV = 2
SPAN = 64
L_DEV = 512
HV = 32
HK = 16
SEQ = 16384
T_DEV = 32
EXPERTS = 64
CAP = 6


def draw_key_proj(key, part):
    key = jax.random.fold_in(key, 11)
    scale_key, base_key = jax.random.split(key)
    channel_scale = jnp.exp(jax.random.uniform(scale_key, (HK * DK,), jnp.float32, math.log(0.03), 0.0))
    base = jax.random.truncated_normal(base_key, -6.0, 6.0, (SEQ, HK * DK), jnp.float32)
    return (base * channel_scale[None, :]).astype(jnp.bfloat16)


def draw_log_decay(key, part):
    key = jax.random.fold_in(key, 23)
    subkeys = jax.random.split(key, 7)
    share_fast = 0.5
    fast = jax.random.uniform(subkeys[0], (HV,), jnp.float32) < share_fast
    fast_rate = jnp.exp(jax.random.uniform(subkeys[1], (HV,), jnp.float32, math.log(1.0 / 50.0), math.log(1.0 / 25.0)))
    slow_rate = jnp.exp(jax.random.uniform(subkeys[2], (HV,), jnp.float32, math.log(0.1), math.log(0.5))) / SEQ
    rate = jnp.where(fast, fast_rate, slow_rate)
    blocks = SEQ // L_DEV
    block_factor = jnp.exp(jax.random.uniform(subkeys[3], (HV, blocks), jnp.float32, -0.7, 0.7))
    rough = jax.random.uniform(subkeys[4], (HV, SEQ), jnp.float32, 0.5, 1.5)
    logarithm_count = -rate[:, None] * jnp.repeat(block_factor, L_DEV, axis=1) * rough
    spots = jax.random.randint(subkeys[5], (HV, 4), 0, SEQ)
    depth = jnp.log(jax.random.uniform(subkeys[6], (HV, 4), jnp.float32, 0.5, 0.8))
    positions = jnp.arange(SEQ, dtype=jnp.int32)
    struck = positions[None, None, :] == spots[:, :, None]
    logarithm_count = logarithm_count + jnp.sum(jnp.where(struck, depth[:, :, None], 0.0), 1)
    return logarithm_count.astype(jnp.float32)


def steps_of(stream_key, extent, cuts, least, top_value):
    level, own = 1.0, jax.random.fold_in(stream_key, 6)
    for axis_at, parts in cuts:
        steps = jnp.exp(jax.random.uniform(jax.random.fold_in(own, axis_at), (parts,), jnp.float32, least / len(cuts), top_value / len(cuts)))
        level = level * jnp.repeat(steps, extent[axis_at] // parts).reshape([-1 if axis == axis_at else 1 for axis in range(len(extent))])
    return level


def shared_out(rng, own, number, rows, amount, top, bound, skew):
    sequence = jax.random.permutation(rng, amount)
    crowded, common = load_shares(amount, rows * top, bound, skew, True), load_shares(amount, rows * top, bound, skew, False)
    places = jnp.arange(amount)

    def named(tallies, rotation):
        used = int((tallies > 0).sum())
        fixed = max(1, used // 4)
        shifted = fixed + (places - fixed + rotation * (used - fixed)) % max(1, amount - fixed)
        return jnp.zeros((amount,), jnp.int32).at[sequence[jnp.where(places < fixed, places, shifted)]].set(jnp.asarray(tallies, jnp.int32))

    tallies = jnp.where(number % 4 == 0, named(crowded, number // 4), named(common, number - number // 4 - 1))
    mixed = jax.random.permutation(jax.random.fold_in(own, 3), amount)
    source_of, receiver = mixed[0:amount // 2 * 2:2], mixed[1:amount // 2 * 2:2]
    slack = jnp.minimum(tallies[source_of] - 1, bound - tallies[receiver]) // 2
    slack = jnp.where((source_of == sequence[0]) | (receiver == sequence[0]) | (tallies[receiver] == 0), 0, jnp.maximum(slack, 0))
    shifted = jax.random.randint(jax.random.fold_in(own, 4), (amount // 2,), 0, 1 << 20) % (slack + 1)
    tallies = tallies.at[source_of].add(-shifted).at[receiver].add(shifted)
    items = jnp.searchsorted(jnp.cumsum(tallies), jnp.arange(rows * top), side="right").astype(jnp.int32)
    table = items.reshape(top, rows).T
    table = table[jax.random.permutation(jax.random.fold_in(own, 1), rows)]
    rotation = jax.random.randint(jax.random.fold_in(own, 2), (rows, 1), 0, top)
    return jnp.take_along_axis(table, (jnp.arange(top)[None, :] + rotation) % top, axis=1)


def load_shares(amount, total, reach, lean, full):
    portions = [(1 << 20) // math.isqrt(rank ** lean) + 1 for rank in range(1, amount + 1)]
    largest = reach if full else min(reach, max(-(-total // amount), total * portions[0] // sum(portions)))
    least = 1 if total - largest >= amount - 1 else 0
    given, surplus = [largest] + [least] * (amount - 1), total - largest - least * (amount - 1)
    while surplus > 0:
        free = [i for i in range(1, amount) if given[i] < largest] or [i for i in range(1, amount) if given[i] < reach]
        whole, left = sum([portions[i] for i in free]), surplus
        for i in free:
            extra = min(reach - given[i], max(1, left * portions[i] // whole), surplus)
            given[i] = given[i] + extra
            surplus = surplus - extra
    return np.array(given)


def normal_values(own_key, dims, deviation, limit, cuts=(), held_as=jnp.bfloat16):
    values = deviation * jax.random.normal(own_key, dims, jnp.float32)
    if cuts:
        values = values * steps_of(own_key, dims, cuts, -0.22, 0.18)
    return jnp.clip(values, -limit, limit).astype(held_as)


def setup_inputs(seed: int = 0) -> dict:
    keys = jax.random.split(jax.random.key(seed), 16)
    query_proj = normal_values(keys[0], (SEQ, HK * DK), 1.0, 6.0, ((0, 32), (1, 16)))
    key_proj = draw_key_proj(jax.random.fold_in(keys[15], 71), 0)
    value_proj = normal_values(keys[2], (SEQ, HV * DV), 1.0, 6.0, ((0, 32), (1, 16)))
    output_gate = normal_values(keys[3], (SEQ, HV * DV), 1.0, 6.0, ((0, 32), (1, 16)))
    beta_logit = normal_values(keys[4], (HV, SEQ), 1.0, 6.0, ((0, 16), (1, 32)), jnp.float32)
    log_decay = draw_log_decay(jax.random.fold_in(keys[15], 71), 0)
    norm_gain = jnp.clip(1.0 + 0.18 * jax.random.normal(keys[6], (DV,), jnp.float32), 0.1, 1.9)
    out_weight = normal_values(keys[7], (HV * DV, D), (HV * DV) ** -0.5, 0.09375, ((0, 16),))
    residual = normal_values(keys[8], (SEQ, D), 1.0, 6.0, ((0, 512),))
    moe_gain = jnp.clip(1.0 + 0.18 * jax.random.normal(keys[9], (D,), jnp.float32), 0.1, 1.9)
    expert_ids_keys = jax.random.split(jax.random.fold_in(keys[10], 1), SEQ // T_DEV)
    expert_ids_turns = jax.random.permutation(jax.random.fold_in(keys[10], 3), SEQ // T_DEV)
    expert_ids = jax.vmap(lambda own, number: shared_out(jax.random.fold_in(keys[10], 2), own, number, T_DEV, EXPERTS, TOPK, CAP, 2))(expert_ids_keys, expert_ids_turns).reshape((SEQ, TOPK))
    route_weight = jnp.clip(0.02 + 0.18 * jax.random.uniform(keys[11], (SEQ, TOPK), jnp.float32) ** steps_of(keys[11], (SEQ, TOPK), ((0, 512),), -0.2, 0.2), 0.02, 0.2)
    expert_gate = normal_values(keys[12], (EXPERTS, D, FH), D ** -0.5, 0.125, ((0, 32), (1, 16)))
    expert_up = normal_values(keys[13], (EXPERTS, D, FH), D ** -0.5, 0.125, ((0, 32), (1, 16)))
    expert_down = normal_values(keys[14], (EXPERTS, FH, D), FH ** -0.5, 0.25, ((0, 32), (2, 16)))
    return dict(query_proj=query_proj, key_proj=key_proj, value_proj=value_proj, output_gate=output_gate, beta_logit=beta_logit, log_decay=log_decay, norm_gain=norm_gain, out_weight=out_weight, residual=residual, moe_gain=moe_gain, expert_ids=expert_ids, route_weight=route_weight, expert_gate=expert_gate, expert_up=expert_up, expert_down=expert_down)


largest_score = lax.Precision.HIGHEST

def normalize_rows(values):
    values = values.astype(jnp.float32)
    return values / jnp.sqrt(lax.optimization_barrier(jnp.sum(values * values, -1, keepdims=True)) + 1e-06)

def unit_lower_inverse(lower_part):
    length = lower_part.shape[0]
    identity = jnp.eye(length, dtype=jnp.float32)
    result = identity - lower_part
    power_term = jnp.dot(lower_part, lower_part, precision=largest_score)
    for _ in range((length - 1).bit_length() - 1):
        result = jnp.dot(result, identity + power_term, precision=largest_score)
        power_term = jnp.dot(power_term, power_term, precision=largest_score)
    return result

def span_step(carry_state, pieces):
    queries, key_rows, values, strength, logarithm_count = pieces
    length = queries.shape[0]
    cumulative = jnp.cumsum(logarithm_count)
    gap_logs = cumulative[:, None] - cumulative[None, :]
    row_index = lax.broadcasted_iota(jnp.int32, (length, length), 0)
    col_index = lax.broadcasted_iota(jnp.int32, (length, length), 1)
    within = row_index >= col_index
    decay_mask = jnp.where(within, jnp.exp(jnp.where(within, gap_logs, 0.0)), 0.0)
    strict = jnp.where(row_index > col_index, decay_mask, 0.0)
    lower_part = jnp.dot(key_rows, key_rows.T, precision=largest_score) * strict * strength[None, :]
    start_scale = jnp.exp(cumulative)
    right_side = values - start_scale[:, None] * jnp.dot(key_rows, carry_state, precision=largest_score)
    update = jnp.dot(unit_lower_inverse(lower_part), right_side, precision=largest_score)
    scores = jnp.dot(queries, key_rows.T, precision=largest_score) * decay_mask * strength[None, :]
    output = start_scale[:, None] * jnp.dot(queries, carry_state, precision=largest_score)
    output = output + jnp.dot(scores, update, precision=largest_score)
    tail_weight = jnp.exp(cumulative[-1] - cumulative) * strength
    carry_state = jnp.exp(cumulative[-1]) * carry_state + jnp.dot((key_rows * tail_weight[:, None]).T, update, precision=largest_score)
    return (carry_state, output)

def delta_rule(queries, key_rows, values, strength, logarithm_count, start):
    length = queries.shape[0]
    blocks = length // SPAN
    pieces = (queries.reshape(blocks, SPAN, -1), key_rows.reshape(blocks, SPAN, -1), values.reshape(blocks, SPAN, -1), strength.reshape(blocks, SPAN), logarithm_count.reshape(blocks, SPAN))
    final, outputs = lax.scan(span_step, start, pieces)
    return (final, outputs.reshape(length, -1))

def reference(query_proj, key_proj, value_proj, output_gate, beta_logit, log_decay, norm_gain, out_weight, residual, moe_gain, expert_ids, route_weight, expert_gate, expert_up, expert_down):
    seq_len = query_proj.shape[0]
    key_heads = query_proj.shape[1] // DK
    value_heads = value_proj.shape[1] // DV
    queries = normalize_rows(query_proj.reshape(seq_len, key_heads, DK)) * DK ** (-0.5)
    key_rows = normalize_rows(key_proj.reshape(seq_len, key_heads, DK))
    ratio = value_heads // key_heads
    queries = jnp.repeat(jnp.transpose(queries, (1, 0, 2)), ratio, axis=0)
    key_rows = jnp.repeat(jnp.transpose(key_rows, (1, 0, 2)), ratio, axis=0)
    values = jnp.transpose(value_proj.reshape(seq_len, value_heads, DV).astype(jnp.float32), (1, 0, 2))
    strength = jax.nn.sigmoid(beta_logit)
    start = jnp.zeros((DK, DV), jnp.float32)
    final, blended_output = jax.vmap(delta_rule, in_axes=(0, 0, 0, 0, 0, None))(queries, key_rows, values, strength, log_decay, start)
    normed_heads = blended_output * lax.rsqrt(lax.optimization_barrier(jnp.mean(blended_output * blended_output, -1, keepdims=True)) + 1e-06) * norm_gain
    gates = jnp.transpose(output_gate.reshape(seq_len, value_heads, DV).astype(jnp.float32), (1, 0, 2))
    gated = (normed_heads * jax.nn.silu(gates)).astype(jnp.bfloat16)
    gated = jnp.transpose(gated, (1, 0, 2)).reshape(seq_len, value_heads * DV)
    group_width = HV_DEV * DV

    def add_group(group_index, accum):
        begin = (group_index * group_width).astype(jnp.int32)
        part = lax.dynamic_slice_in_dim(gated, begin, group_width, 1)
        weights = lax.dynamic_slice_in_dim(out_weight, begin, group_width, 0)
        term = jnp.dot(part, weights, preferred_element_type=jnp.float32).astype(jnp.bfloat16)
        return accum + lax.optimization_barrier(term).astype(jnp.float32)
    attended = lax.fori_loop(0, value_heads // HV_DEV, add_group, jnp.zeros((seq_len, D), jnp.float32))
    hidden = residual.astype(jnp.float32) + attended
    normed = (hidden * lax.rsqrt(lax.optimization_barrier(jnp.mean(hidden * hidden, -1, keepdims=True)) + 1e-06) * moe_gain).astype(jnp.bfloat16)
    total_experts = expert_gate.shape[0]
    limit_rows = seq_len // T_DEV * CAP
    token_index = jnp.arange(seq_len, dtype=jnp.int32)

    def per_expert(accum, expert):
        hit = expert_ids == expert
        weight = lax.optimization_barrier(jnp.sum(jnp.where(hit, route_weight, 0.0), -1))
        selected_experts = jnp.any(hit, -1)
        place = jnp.cumsum(selected_experts.astype(jnp.int32)) - 1
        target = jnp.where(selected_experts, place, limit_rows).astype(jnp.int32)
        table = jnp.full((limit_rows,), seq_len, jnp.int32).at[target].set(token_index, mode='drop')
        rows = jnp.take(normed, table, axis=0, mode='fill', fill_value=0)
        first = jnp.dot(rows, expert_gate[expert], preferred_element_type=jnp.float32)
        second = jnp.dot(rows, expert_up[expert], preferred_element_type=jnp.float32)
        inner = (jax.nn.silu(first) * second).astype(jnp.bfloat16)
        final_result = jnp.dot(inner, expert_down[expert], preferred_element_type=jnp.float32).astype(jnp.bfloat16)
        scale_rows = jnp.take(weight, table, axis=0, mode='fill', fill_value=0)
        accum = accum.at[table].add(final_result.astype(jnp.float32) * scale_rows[:, None], mode='drop')
        return (accum, None)
    mixture, unused = lax.scan(per_expert, jnp.zeros((seq_len, D), jnp.float32), jnp.arange(total_experts, dtype=jnp.int32))
    return (hidden + mixture).astype(jnp.bfloat16)
```

```python
import functools

import jax
import jax.numpy as jnp
from jax import lax
from jax.experimental import pallas as pl
from jax.experimental.pallas import tpu as pltpu
from jax.sharding import PartitionSpec as P

BLOCK = 128
f32 = jnp.float32
bf16 = jnp.bfloat16
VMEM = pltpu.VMEM
SMEM = pltpu.SMEM
MIB = 1 << 20


def vmem():
    return pl.BlockSpec(memory_space=VMEM)


def smem():
    return pl.BlockSpec(memory_space=SMEM)


def params(mib):
    return pltpu.CompilerParams(vmem_limit_bytes=mib * MIB)


def cost(flops, moved):
    return pl.CostEstimate(flops=int(flops), bytes_accessed=int(moved), transcendentals=0)


def mm(left, right):
    return jnp.dot(left.astype(bf16), right.astype(bf16), preferred_element_type=f32)


def mm_nt(left, right):
    return lax.dot_general(
        left.astype(bf16),
        right.astype(bf16),
        (((1,), (1,)), ((), ())),
        preferred_element_type=f32,
    )


def sigmoid(value):
    return 1.0 / (1.0 + jnp.exp(-value))


def scan_kernel(heads, q_ref, k_ref, v_ref, beta_ref, log_ref, carry_ref, blend_ref, own_ref):
    length, dk = q_ref.shape
    count = length // BLOCK
    row = lax.broadcasted_iota(jnp.int32, (BLOCK, BLOCK), 0)
    col = lax.broadcasted_iota(jnp.int32, (BLOCK, BLOCK), 1)
    problems = []
    for c in range(count):
        span = slice(c * BLOCK, (c + 1) * BLOCK)
        keys, queries = k_ref[span, :], q_ref[span, :]
        key_values, query_values = keys.astype(f32), queries.astype(f32)
        key_scale = lax.rsqrt(jnp.sum(key_values * key_values, 1, keepdims=True) + 1e-06)
        query_scale = lax.rsqrt(
            jnp.sum(query_values * query_values, 1, keepdims=True) + 1e-06
        ) * dk ** (-0.5)
        key_scale_row = jnp.sum(jnp.where(row == col, key_scale, 0.0), 0, keepdims=True)
        key_key = mm_nt(keys, keys) * key_scale * key_scale_row
        query_key = mm_nt(queries, keys) * query_scale * key_scale_row
        keys_t = jnp.transpose(key_values)
        for h in range(heads):
            logs = log_ref[h : h + 1, span]
            beta = sigmoid(beta_ref[h : h + 1, span])
            logs_col = jnp.sum(jnp.where(row == col, logs, 0.0), 1, keepdims=True)
            total_row = jnp.sum(jnp.where(row <= col, logs_col, 0.0), 0, keepdims=True)
            total_col = jnp.sum(jnp.where(col <= row, logs, 0.0), 1, keepdims=True)
            within = row >= col
            mask = jnp.where(
                within, jnp.exp(jnp.where(within, total_col - total_row, 0.0)), 0.0
            ) * beta
            lower = jnp.where(row > col, key_key * mask, 0.0)
            end = total_row[:, BLOCK - 1 : BLOCK]
            problems.append(
                dict(
                    lower=lower,
                    inverse=jnp.where(row == col, 1.0, 0.0)
                    - jnp.where(row // 2 == col // 2, lower, 0.0),
                    scores=(query_key * mask).astype(bf16),
                    into=jnp.exp(total_row) * key_scale_row,
                    queries=query_values * (jnp.exp(total_col) * query_scale),
                    tail=(keys_t * (jnp.exp(end - total_row) * beta * key_scale_row)).astype(bf16),
                    gain=jnp.exp(end),
                    keys=keys,
                    values=v_ref[span, h * dk : (h + 1) * dk],
                )
            )
    width = 2
    while width < BLOCK:
        pick = (row // (2 * width) == col // (2 * width)) & (row // width != col // width)
        for p in problems:
            inverse = p["inverse"].astype(bf16)
            step = mm(inverse, jnp.where(pick, p["lower"], 0.0))
            p["inverse"] = p["inverse"] - mm(step, inverse)
        width *= 2
    for p in problems:
        p["both"] = jnp.concatenate(
            [mm(p["inverse"] * p["into"], p["keys"]), mm(p["inverse"], p["values"])], 1
        ).astype(bf16)
    for p in problems:
        p["seen"] = mm(p["scores"], p["both"])
        p["push"] = mm(p["tail"], p["both"])
    states = []
    for h in range(heads):
        states.append(
            jnp.concatenate(
                [jnp.where(row == col, 1.0, 0.0), jnp.zeros((dk, dk), f32)], 1
            )
        )
    for c in range(count):
        span = slice(c * BLOCK, (c + 1) * BLOCK)
        for h in range(heads):
            p = problems[c * heads + h]
            state = states[h]
            low = state.astype(bf16)
            out = mm(p["queries"] - p["seen"][:, :dk], low)
            blend_ref[h, span, :] = out[:, :dk].astype(bf16)
            own_ref[h, span, :] = out[:, dk:] + p["seen"][:, dk:]
            push = p["push"]
            moved = mm(push[:, :dk], low)
            states[h] = jnp.concatenate(
                [
                    p["gain"] * state[:, :dk] - moved[:, :dk],
                    p["gain"] * state[:, dk:] - moved[:, dk:] + push[:, dk:],
                ],
                1,
            )
    for h in range(heads):
        carry_ref[h, :dk, :] = jnp.transpose(states[h][:, :dk]).astype(bf16)
        carry_ref[h, dk:, :] = jnp.transpose(states[h][:, dk:]).astype(bf16)


def follow(late, early):
    dk = late.shape[-1]
    moved = mm(early, late[:dk])
    return jnp.concatenate([moved[:dk], moved[dk:] + late[dk:].astype(f32)], 0).astype(bf16)


def row_kernel(where_ref, m0, m1, m2, m3, total_ref, before_ref):
    x = where_ref[0]
    maps = (m0, m1, m2, m3)
    heads, _, dk = m0.shape
    half = dk * heads // 4
    for place in range(4):

        @pl.when(x == place)
        def _():
            ordered = [maps[(place - j) % 4] for j in range(4)]
            for h in range(heads):
                parts = [ordered[j][h] for j in range(4)]
                prefix = parts[0]
                for j in range(1, place):
                    prefix = follow(parts[j], prefix)
                if place == 0:
                    eye = lax.broadcasted_iota(jnp.int32, (dk, dk), 0) == (
                        lax.broadcasted_iota(jnp.int32, (dk, dk), 1)
                    )
                    prefix = jnp.concatenate(
                        [jnp.where(eye, 1.0, 0.0), jnp.zeros((dk, dk), f32)], 0
                    ).astype(bf16)
                before_ref[h] = prefix
                if h == place // 2:
                    low = dk + (place % 2) * half
                    cut = [
                        jnp.concatenate([part[:dk], part[low : low + half]], 0) for part in parts
                    ]
                    total = cut[0]
                    for j in range(1, 4):
                        total = follow(cut[j], total)
                    total_ref[...] = total


def state_kernel(where_ref, s0, s1, s2, s3, before_ref, out_ref, scratch):
    x = where_ref[0]
    heads, _, dk = before_ref.shape
    for k, part in enumerate((s0, s1, s2, s3)):
        scratch[lax.rem(x - k + 4, 4)] = part[...]
    for h in range(heads):
        row_state = jnp.concatenate([scratch[2 * h], scratch[2 * h + 1]], 0)
        moved = mm(row_state, before_ref[h, :dk, :])
        out_ref[h] = (moved + before_ref[h, dk:, :].astype(f32)).astype(bf16)


def gate_kernel(
    where_ref, s0, s1, s2, s3, before_ref, blend_ref, own_ref, gate_ref, gain_ref, out_ref,
    quarters, entry,
):
    state_kernel(where_ref, s0, s1, s2, s3, before_ref, entry, quarters)
    core = where_ref[1]
    heads, length, dk = own_ref.shape
    pairs, tokens = out_ref.shape[1], out_ref.shape[2]
    gain = gain_ref[...]
    for h in range(heads):
        mixed = own_ref[h] + mm_nt(blend_ref[h], entry[h])
        scale = lax.rsqrt(jnp.mean(mixed * mixed, 1, keepdims=True) + 1e-06)
        gates = gate_ref[:, h * dk : (h + 1) * dk].astype(f32)
        gated = (mixed * scale * gain * (gates * sigmoid(gates))).astype(bf16)
        for parity in range(2):
            mine = lax.rem(parity + core, 2)
            for pair in range(pairs):
                start = (2 * pair + parity) * tokens
                out_ref[mine, pair, :, h * dk : (h + 1) * dk] = gated[start : start + tokens]


def project_kernel(kept_ref, got_ref, own_ref, other_ref, out_ref):
    pairs, tokens, width = got_ref.shape
    rows = pairs * tokens
    total = mm(kept_ref[0].reshape(rows, width), own_ref[...])
    total = total + mm(got_ref[...].reshape(rows, width), other_ref[...])
    out_ref[...] = total.astype(bf16).reshape(out_ref.shape)


def route_kernel(topk, capacity, ids_ref, slot_ref, owner_ref, count_ref):
    tokens = ids_ref.shape[0]
    experts = count_ref.shape[0]

    def clear(i, carry):
        count_ref[i] = 0
        for r in range(capacity):
            owner_ref[i * capacity + r] = 0
        return carry

    lax.fori_loop(0, experts, clear, 0)

    def place(t, carry):
        for k in range(topk):
            expert = ids_ref[t, k]
            rank = count_ref[expert]
            count_ref[expert] = rank + 1
            slot = expert * capacity + rank
            slot_ref[t * topk + k] = slot
            owner_ref[slot] = t
        return carry

    lax.fori_loop(0, tokens, place, 0)


def dispatch_kernel(
    owner_ref, parts_ref, residual_ref, gain_ref, hidden_ref, out_ref, rows_ref, tiles_ref
):
    sources, tokens, width = parts_ref.shape
    lanes = out_ref.shape[2]
    cuts = width // lanes
    hidden = parts_ref[0].astype(f32)
    for s in range(1, sources):
        hidden = hidden + parts_ref[s].astype(f32)
    hidden = hidden + residual_ref[...].astype(f32)
    hidden_ref[...] = hidden
    scale = lax.rsqrt(jnp.mean(hidden * hidden, 1, keepdims=True) + 1e-06)
    normed = hidden * scale * gain_ref[...]
    for j in range(cuts):
        rows_ref[pl.ds(j, tokens, stride=cuts), :] = normed[:, j * lanes : (j + 1) * lanes]
    tiles_ref[...] = rows_ref[...].astype(bf16).reshape(tiles_ref.shape)
    unroll = 8

    def place(i, carry):
        for u in range(unroll):
            slot = i * unroll + u
            out_ref[slot] = tiles_ref[owner_ref[slot]]
        return carry

    lax.fori_loop(0, out_ref.shape[0] // unroll, place, 0)


def expert_kernel(rows_ref, gate_ref, up_ref, down_ref, out_ref, wide, flat):
    groups, _, capacity, cuts, lanes = rows_ref.shape
    rows = groups * capacity
    hidden_units = gate_ref.shape[3]
    depth = cuts * lanes
    wide[...] = rows_ref[...].astype(f32).reshape(rows * cuts, lanes)
    for j in range(cuts):
        flat[:, j * lanes : (j + 1) * lanes] = wide[pl.ds(j, rows, stride=cuts), :].astype(bf16)
    tokens = flat[...]
    first = mm(tokens, gate_ref[...].reshape(depth, hidden_units))
    second = mm(tokens, up_ref[...].reshape(depth, hidden_units))
    inner = (first * sigmoid(first) * second).astype(bf16)
    for j in range(0, cuts, 2):
        columns = []
        for packed in (down_ref[j, 0], down_ref[j + 1, 0]):
            columns.append(
                jnp.concatenate(
                    [packed[:, b : b + lanes] for b in range(0, hidden_units, lanes)], 0
                )
            )
        answer = mm(inner, jnp.concatenate(columns, 1))
        wide[pl.ds(j, rows, stride=cuts), :] = answer[:, :lanes]
        wide[pl.ds(j + 1, rows, stride=cuts), :] = answer[:, lanes:]
    out_ref[...] = wide[...].astype(bf16).reshape(out_ref.shape)


def combine_kernel(topk, slot_ref, weight_ref, back_ref, hidden_ref, out_ref, total):
    tokens, width = hidden_ref.shape
    cuts, lanes = back_ref.shape[1:]

    def add(t, carry):
        acc = jnp.zeros((cuts, lanes), f32)
        for k in range(topk):
            acc = acc + weight_ref[t, k] * back_ref[slot_ref[t * topk + k]].astype(f32)
        total[pl.ds(pl.multiple_of(t * cuts, cuts), cuts), :] = acc
        return carry

    lax.fori_loop(0, tokens, add, 0)
    for j in range(cuts):
        span = slice(j * lanes, (j + 1) * lanes)
        mixture = total[pl.ds(j, tokens, stride=cuts), :]
        out_ref[:, span] = (hidden_ref[:, span] + mixture).astype(bf16)


def shards(
    query_proj,
    key_proj,
    value_proj,
    output_gate,
    beta_logit,
    log_decay,
    norm_gain,
    out_weight,
    residual,
    moe_gain,
    expert_ids,
    route_weight,
    expert_gate,
    expert_up,
    expert_down,
):
    length, dk = query_proj.shape
    heads = beta_logit.shape[0]
    tokens, width = residual.shape
    experts_here, _, hidden_units = expert_gate.shape
    groups = lax.axis_size("ctx")
    topk = expert_ids.shape[1]
    capacity = 6
    lanes = 128
    cuts = width // lanes
    slots = groups * experts_here * capacity
    columns = 4
    pairs = lax.axis_size("exp") // 2
    rows = groups // columns
    place = lax.axis_index("ctx")
    x = lax.rem(place, columns)
    core = lax.rem(lax.axis_index("exp"), 2)
    where = jnp.stack([x, core]).astype(jnp.int32)

    def pair_swap(block):
        return lax.ppermute(block, "exp", [(i, i ^ 1) for i in range(2 * pairs)])

    def along_x(block, k):
        route = [
            (y * columns + i, y * columns + (i + k) % columns)
            for y in range(rows)
            for i in range(columns)
        ]
        return lax.ppermute(block, "ctx", route)

    def along_y(block, k):
        route = [(i, i + k * columns) for i in range((rows - k) * columns)]
        return lax.ppermute(block, "ctx", route)

    down_blocks = jnp.concatenate(
        [expert_down[:, b : b + lanes, :] for b in range(0, hidden_units, lanes)], 2
    )
    packed = jnp.concatenate([expert_gate, expert_up, down_blocks], 0)
    gathered = lax.all_gather(packed, "exp", axis=0)
    other_weight = pair_swap(out_weight)

    slot, owner = pl.pallas_call(
        functools.partial(route_kernel, topk, capacity),
        out_shape=(
            jax.ShapeDtypeStruct((tokens * topk,), jnp.int32),
            jax.ShapeDtypeStruct((slots,), jnp.int32),
        ),
        in_specs=[smem()],
        out_specs=(smem(), smem()),
        scratch_shapes=[pltpu.SMEM((groups * experts_here,), jnp.int32)],
        name="route",
    )(expert_ids)

    carry, blend, own = pl.pallas_call(
        functools.partial(scan_kernel, heads),
        out_shape=(
            jax.ShapeDtypeStruct((heads, 2 * dk, dk), bf16),
            jax.ShapeDtypeStruct((heads, length, dk), bf16),
            jax.ShapeDtypeStruct((heads, length, dk), f32),
        ),
        in_specs=[vmem()] * 5,
        out_specs=(vmem(),) * 3,
        compiler_params=params(32),
        cost_estimate=cost(2e9, 2e6),
        name="scan",
    )(query_proj, key_proj, value_proj, beta_logit, log_decay)

    maps = [carry] + [along_x(carry, k) for k in range(1, columns)]
    half = dk * heads // columns
    total, before = pl.pallas_call(
        row_kernel,
        out_shape=(
            jax.ShapeDtypeStruct((dk + half, dk), bf16),
            jax.ShapeDtypeStruct((heads, 2 * dk, dk), bf16),
        ),
        in_specs=[smem()] + [vmem()] * 4,
        out_specs=(vmem(), vmem()),
        name="row",
    )(where, *maps)
    window = follow(along_y(total, 1), along_y(total, 2))
    window = follow(window, along_y(window, 2))
    arrived = along_y(window[dk:], 4)
    quarter = (mm(arrived, window[:dk]) + window[dk:].astype(f32)).astype(bf16)
    quarters = [quarter] + [along_x(quarter, k) for k in range(1, columns)]

    gated = pl.pallas_call(
        gate_kernel,
        out_shape=jax.ShapeDtypeStruct((2, pairs, tokens, heads * dk), bf16),
        in_specs=[smem()] + [vmem()] * 9,
        out_specs=vmem(),
        scratch_shapes=[
            pltpu.VMEM((columns, half, dk), bf16),
            pltpu.VMEM((heads, dk, dk), bf16),
        ],
        compiler_params=params(32),
        cost_estimate=cost(1e8, 2e6),
        name="gate",
    )(where, *quarters, before, blend, own, output_gate, norm_gain.reshape(1, dk))
    got = pair_swap(gated[1])
    steps = 4
    wide = width // steps
    partial_sums = pl.pallas_call(
        project_kernel,
        grid=(steps,),
        out_shape=jax.ShapeDtypeStruct((pairs, tokens, width), bf16),
        in_specs=[
            pl.BlockSpec((1, pairs, tokens, heads * dk), lambda n: (0, 0, 0, 0)),
            pl.BlockSpec((pairs, tokens, heads * dk), lambda n: (0, 0, 0)),
            pl.BlockSpec((heads * dk, wide), lambda n: (0, n)),
            pl.BlockSpec((heads * dk, wide), lambda n: (0, n)),
        ],
        out_specs=pl.BlockSpec((pairs, tokens, wide), lambda n: (0, 0, n)),
        compiler_params=params(32),
        cost_estimate=cost(6e8, 4e6),
        name="project",
    )(gated, got, out_weight, other_weight)
    same_core = [[c + 2 * z for z in range(pairs)] for c in range(2)]
    parts = lax.all_to_all(
        partial_sums, "exp", 0, 0, tiled=True, axis_index_groups=same_core
    )

    hidden, outgoing = pl.pallas_call(
        dispatch_kernel,
        out_shape=(
            jax.ShapeDtypeStruct((tokens, width), f32),
            jax.ShapeDtypeStruct((slots, cuts, lanes), bf16),
        ),
        in_specs=[smem(), vmem(), vmem(), vmem()],
        out_specs=(vmem(), vmem()),
        scratch_shapes=[
            pltpu.VMEM((tokens * cuts, lanes), f32),
            pltpu.VMEM((tokens, cuts, lanes), bf16),
        ],
        compiler_params=params(32),
        cost_estimate=cost(1e6, 3e6),
        name="dispatch",
    )(owner, parts, residual, moe_gain.reshape(1, width))
    outgoing = outgoing.reshape(groups, experts_here, capacity, cuts, lanes)
    incoming = lax.all_to_all(outgoing, "ctx", 0, 0, tiled=True)

    shape = (groups, 1, capacity, cuts, lanes)
    weights = (2 * pairs, 1) + packed.shape[1:]
    answers = pl.pallas_call(
        expert_kernel,
        grid=(experts_here,),
        out_shape=jax.ShapeDtypeStruct(incoming.shape, bf16),
        in_specs=[
            pl.BlockSpec(shape, lambda e: (0, e, 0, 0, 0)),
            pl.BlockSpec(weights, lambda e: (0, e, 0, 0)),
            pl.BlockSpec(weights, lambda e: (0, experts_here + e, 0, 0)),
            pl.BlockSpec(weights, lambda e: (0, 2 * experts_here + e, 0, 0)),
        ],
        out_specs=pl.BlockSpec(shape, lambda e: (0, e, 0, 0, 0)),
        scratch_shapes=[
            pltpu.VMEM((groups * capacity * cuts, lanes), f32),
            pltpu.VMEM((groups * capacity, width), bf16),
        ],
        compiler_params=params(48),
        cost_estimate=cost(3e9, 16e6),
        name="experts",
    )(incoming, gathered, gathered, gathered)
    returned = lax.all_to_all(answers, "ctx", 0, 0, tiled=True).reshape(slots, cuts, lanes)

    return pl.pallas_call(
        functools.partial(combine_kernel, topk),
        out_shape=jax.ShapeDtypeStruct((tokens, width), bf16),
        in_specs=[smem(), smem(), vmem(), vmem()],
        out_specs=vmem(),
        scratch_shapes=[pltpu.VMEM((tokens * cuts, lanes), f32)],
        compiler_params=params(32),
        cost_estimate=cost(1e6, 3e6),
        name="combine",
    )(slot, route_weight, returned, hidden)


def solution(mesh):
    placed = (
        P("ctx", "exp"),
        P("ctx", "exp"),
        P("ctx", "exp"),
        P("ctx", "exp"),
        P("exp", "ctx"),
        P("exp", "ctx"),
        P(),
        P("exp", None),
        P(("ctx", "exp"), None),
        P(),
        P(("ctx", "exp"), None),
        P(("ctx", "exp"), None),
        P("ctx", "exp", None),
        P("ctx", "exp", None),
        P("ctx", None, "exp"),
    )
    return jax.shard_map(
        shards, mesh=mesh, in_specs=placed, out_specs=P(("ctx", "exp"), None), check_vma=False
    )
```

```python
import functools

import jax
import jax.numpy as jnp
from jax import lax
from jax.experimental import pallas as pl
from jax.experimental.pallas import tpu as pltpu
from jax.sharding import PartitionSpec as P

BLOCK = 128
f32 = jnp.float32
bf16 = jnp.bfloat16
VMEM = pltpu.VMEM
SMEM = pltpu.SMEM
MIB = 1 << 20


def vmem():
    return pl.BlockSpec(memory_space=VMEM)


def smem():
    return pl.BlockSpec(memory_space=SMEM)


def anywhere():
    return pl.BlockSpec(memory_space=pl.ANY)


def params(mib):
    return pltpu.CompilerParams(vmem_limit_bytes=mib * MIB)


def cost(flops, moved):
    return pl.CostEstimate(flops=int(flops), bytes_accessed=int(moved), transcendentals=0)


def mm(left, right):
    return jnp.dot(left.astype(bf16), right.astype(bf16), preferred_element_type=f32)


def mm_nt(left, right):
    return lax.dot_general(
        left.astype(bf16),
        right.astype(bf16),
        (((1,), (1,)), ((), ())),
        preferred_element_type=f32,
    )


def sigmoid(value):
    return 1.0 / (1.0 + jnp.exp(-value))


def start_copies(moves, sems):
    copies = [pltpu.make_async_copy(a, b, sems.at[i]) for i, (a, b) in enumerate(moves)]
    for copy in copies:
        copy.start()
    return copies


def pack_down(down_ref, packed_ref):
    experts, depth, lanes = down_ref.shape
    return [
        (down_ref.at[e, b : b + lanes, :], packed_ref.at[e, :, b : b + lanes])
        for e in range(experts)
        for b in range(0, depth, lanes)
    ]


def scan_kernel(
    heads, q_ref, k_ref, v_ref, beta_ref, log_ref, gate_ref, up_ref,
    carry_ref, blend_ref, own_ref, packed_ref, sems,
):
    experts = gate_ref.shape[0]
    copies = start_copies(
        [(gate_ref, packed_ref.at[0:experts]), (up_ref, packed_ref.at[experts : 2 * experts])],
        sems,
    )
    length, dk = q_ref.shape
    count = length // BLOCK
    row = lax.broadcasted_iota(jnp.int32, (BLOCK, BLOCK), 0)
    col = lax.broadcasted_iota(jnp.int32, (BLOCK, BLOCK), 1)
    problems = []
    for c in range(count):
        span = slice(c * BLOCK, (c + 1) * BLOCK)
        keys, queries = k_ref[span, :], q_ref[span, :]
        key_values, query_values = keys.astype(f32), queries.astype(f32)
        key_scale = lax.rsqrt(jnp.sum(key_values * key_values, 1, keepdims=True) + 1e-06)
        query_scale = lax.rsqrt(
            jnp.sum(query_values * query_values, 1, keepdims=True) + 1e-06
        ) * dk ** (-0.5)
        key_scale_row = jnp.sum(jnp.where(row == col, key_scale, 0.0), 0, keepdims=True)
        key_key = mm_nt(keys, keys) * key_scale * key_scale_row
        query_key = mm_nt(queries, keys) * query_scale * key_scale_row
        keys_t = jnp.transpose(key_values)
        for h in range(heads):
            logs = log_ref[h : h + 1, span]
            beta = sigmoid(beta_ref[h : h + 1, span])
            logs_col = jnp.sum(jnp.where(row == col, logs, 0.0), 1, keepdims=True)
            total_row = jnp.sum(jnp.where(row <= col, logs_col, 0.0), 0, keepdims=True)
            total_col = jnp.sum(jnp.where(col <= row, logs, 0.0), 1, keepdims=True)
            within = row >= col
            mask = jnp.where(
                within, jnp.exp(jnp.where(within, total_col - total_row, 0.0)), 0.0
            ) * beta
            lower = jnp.where(row > col, key_key * mask, 0.0)
            end = total_row[:, BLOCK - 1 : BLOCK]
            problems.append(
                dict(
                    lower=lower,
                    inverse=jnp.where(row == col, 1.0, 0.0)
                    - jnp.where(row // 2 == col // 2, lower, 0.0),
                    scores=(query_key * mask).astype(bf16),
                    into=jnp.exp(total_row) * key_scale_row,
                    queries=query_values * (jnp.exp(total_col) * query_scale),
                    tail=(keys_t * (jnp.exp(end - total_row) * beta * key_scale_row)).astype(bf16),
                    gain=jnp.exp(end),
                    keys=keys,
                    values=v_ref[span, h * dk : (h + 1) * dk],
                )
            )
    width = 2
    while width < BLOCK:
        pick = (row // (2 * width) == col // (2 * width)) & (row // width != col // width)
        for p in problems:
            inverse = p["inverse"].astype(bf16)
            step = mm(inverse, jnp.where(pick, p["lower"], 0.0))
            p["inverse"] = p["inverse"] - mm(step, inverse)
        width *= 2
    for p in problems:
        p["both"] = jnp.concatenate(
            [mm(p["inverse"] * p["into"], p["keys"]), mm(p["inverse"], p["values"])], 1
        ).astype(bf16)
    for p in problems:
        p["seen"] = mm(p["scores"], p["both"])
        p["push"] = mm(p["tail"], p["both"])
    states = []
    for h in range(heads):
        states.append(
            jnp.concatenate(
                [jnp.where(row == col, 1.0, 0.0), jnp.zeros((dk, dk), f32)], 1
            )
        )
    for c in range(count):
        span = slice(c * BLOCK, (c + 1) * BLOCK)
        for h in range(heads):
            p = problems[c * heads + h]
            state = states[h]
            low = state.astype(bf16)
            out = mm(p["queries"] - p["seen"][:, :dk], low)
            blend_ref[h, span, :] = out[:, :dk].astype(bf16)
            own_ref[h, span, :] = (out[:, dk:] + p["seen"][:, dk:]).astype(bf16)
            push = p["push"]
            moved = mm(push[:, :dk], low)
            states[h] = jnp.concatenate(
                [
                    p["gain"] * state[:, :dk] - moved[:, :dk],
                    p["gain"] * state[:, dk:] - moved[:, dk:] + push[:, dk:],
                ],
                1,
            )
    for h in range(heads):
        for part in range(2):
            turned = jnp.transpose(states[h][:, part * dk : (part + 1) * dk]).astype(bf16)
            for place in range(carry_ref.shape[0]):
                carry_ref[place, h, part * dk : (part + 1) * dk, :] = turned
    for copy in copies:
        copy.wait()


def follow(late, early):
    dk = late.shape[-1]
    moved = mm(early, late[:dk])
    return jnp.concatenate([moved[:dk], moved[dk:] + late[dk:].astype(f32)], 0).astype(bf16)


def row_kernel(maps_ref, total_ref, before_ref):
    columns, heads, _, dk = maps_ref.shape
    x = lax.rem(lax.axis_index("ctx"), columns)
    half = dk * heads // columns
    for place in range(columns):

        @pl.when(x == place)
        def _():
            for h in range(heads):
                parts = [maps_ref[j, h] for j in range(columns)]
                prefix = parts[0]
                for j in range(1, place):
                    prefix = follow(parts[j], prefix)
                if place == 0:
                    eye = lax.broadcasted_iota(jnp.int32, (dk, dk), 0) == (
                        lax.broadcasted_iota(jnp.int32, (dk, dk), 1)
                    )
                    prefix = jnp.concatenate(
                        [jnp.where(eye, 1.0, 0.0), jnp.zeros((dk, dk), f32)], 0
                    ).astype(bf16)
                before_ref[h] = prefix
                if h == place * heads // columns:
                    low = dk + (place % (columns // heads)) * half
                    cut = [
                        jnp.concatenate([part[:dk], part[low : low + half]], 0) for part in parts
                    ]
                    total = cut[0]
                    for j in range(1, columns):
                        total = follow(cut[j], total)
                    for row in range(total_ref.shape[0]):
                        total_ref[row] = total


def column_kernel(totals_ref, out_ref):
    dk = totals_ref.shape[2]
    y = lax.axis_index("ctx") // out_ref.shape[0]

    state = jnp.zeros(out_ref.shape[1:], f32)
    for j in range(totals_ref.shape[0] - 1):
        moved = mm(state, totals_ref[j, :dk, :]) + totals_ref[j, dk:, :].astype(f32)
        state = jnp.where(j < y, moved, state)
    state = state.astype(bf16)
    for place in range(out_ref.shape[0]):
        out_ref[place] = state


def gate_kernel(
    quarters_ref, before_ref, blend_ref, own_ref, gate_ref, gain_ref, out_ref
):
    core = lax.rem(lax.axis_index("exp"), 2)
    heads, length, dk = own_ref.shape
    pairs, tokens = out_ref.shape[1], out_ref.shape[2]
    share = quarters_ref.shape[0] // heads
    gain = gain_ref[...]
    for h in range(heads):
        row_state = jnp.concatenate([quarters_ref[share * h + i] for i in range(share)], 0)
        entry = mm(row_state, before_ref[h, :dk, :]) + before_ref[h, dk:, :].astype(f32)
        mixed = own_ref[h].astype(f32) + mm_nt(blend_ref[h], entry)
        scale = lax.rsqrt(jnp.mean(mixed * mixed, 1, keepdims=True) + 1e-06)
        gates = gate_ref[:, h * dk : (h + 1) * dk].astype(f32)
        gated = (mixed * scale * gain * (gates * sigmoid(gates))).astype(bf16)
        for parity in range(2):
            mine = lax.rem(parity + core, 2)
            for pair in range(pairs):
                start = (2 * pair + parity) * tokens
                out_ref[mine, pair, :, h * dk : (h + 1) * dk] = gated[start : start + tokens]


def project_kernel(kept_ref, got_ref, own_ref, other_ref, out_ref):
    pairs, tokens, width = got_ref.shape
    rows = pairs * tokens
    total = mm(kept_ref[0].reshape(rows, width), own_ref[...])
    total = total + mm(got_ref[...].reshape(rows, width), other_ref[...])
    out_ref[...] = total.astype(bf16).reshape(out_ref.shape)


def route_kernel(topk, capacity, ids_ref, slot_ref, owner_ref, count_ref):
    tokens = ids_ref.shape[0]
    experts = count_ref.shape[0]

    def clear(i, carry):
        count_ref[i] = 0
        for r in range(capacity):
            owner_ref[i * capacity + r] = 0
        return carry

    lax.fori_loop(0, experts, clear, 0)

    def place(t, carry):
        for k in range(topk):
            expert = ids_ref[t, k]
            rank = count_ref[expert]
            count_ref[expert] = rank + 1
            slot = expert * capacity + rank
            slot_ref[t * topk + k] = slot
            owner_ref[slot] = t
        return carry

    lax.fori_loop(0, tokens, place, 0)


def dispatch_kernel(
    owner_ref, parts_ref, residual_ref, gain_ref, down_ref, after_ref,
    hidden_ref, out_ref, packed_ref, rows_ref, tiles_ref, sems,
):
    copies = start_copies(pack_down(down_ref, packed_ref), sems)
    sources, tokens, width = parts_ref.shape
    lanes = out_ref.shape[2]
    cuts = width // lanes
    hidden = parts_ref[0].astype(f32)
    for s in range(1, sources):
        hidden = hidden + parts_ref[s].astype(f32)
    hidden = hidden + residual_ref[...].astype(f32)
    hidden_ref[...] = hidden
    scale = lax.rsqrt(jnp.mean(hidden * hidden, 1, keepdims=True) + 1e-06)
    normed = hidden * scale * gain_ref[...]
    for j in range(cuts):
        rows_ref[pl.ds(j, tokens, stride=cuts), :] = normed[:, j * lanes : (j + 1) * lanes]
    tiles_ref[...] = rows_ref[...].astype(bf16).reshape(tiles_ref.shape)
    unroll = 8

    def place(i, carry):
        for u in range(unroll):
            slot = i * unroll + u
            out_ref[slot] = tiles_ref[owner_ref[slot]]
        return carry

    lax.fori_loop(0, out_ref.shape[0] // unroll, place, 0)
    for copy in copies:
        copy.wait()


def expert_kernel(rows_ref, first_ref, last_ref, out_ref, first_vmem, last_vmem, sems, *scratch):
    groups, experts, capacity, cuts, lanes = rows_ref.shape
    moves = []
    for e in range(experts):
        moves.append((first_ref.at[:, e], first_vmem.at[:, e]))
        moves.append((first_ref.at[:, experts + e], first_vmem.at[:, experts + e]))
        moves.append((last_ref.at[:, e], last_vmem.at[:, e]))
    copies = start_copies(moves, sems)
    rows = groups * capacity
    hidden_units = first_ref.shape[3]
    depth = cuts * lanes
    wide_in, wide_out, flat = scratch[:experts], scratch[experts : 2 * experts], scratch[2 * experts :]
    for e in range(experts):
        wide_in[e][...] = rows_ref[:, e].astype(f32).reshape(rows * cuts, lanes)
        for j in range(cuts):
            part = wide_in[e][pl.ds(j, rows, stride=cuts), :]
            flat[e][:, j * lanes : (j + 1) * lanes] = part.astype(bf16)
    for e in range(experts):
        tokens = flat[e][...]
        copies[3 * e].wait()
        first = mm(tokens, first_vmem[:, e].reshape(depth, hidden_units))
        copies[3 * e + 1].wait()
        second = mm(tokens, first_vmem[:, experts + e].reshape(depth, hidden_units))
        inner = (first * sigmoid(first) * second).astype(bf16)
        copies[3 * e + 2].wait()
        for j in range(0, cuts, 2):
            columns = []
            for k in (j, j + 1):
                columns.append(
                    jnp.concatenate(
                        [
                            last_vmem[k, e, :, b : b + lanes]
                            for b in range(0, hidden_units, lanes)
                        ],
                        0,
                    )
                )
            answer = mm(inner, jnp.concatenate(columns, 1))
            wide_out[e][pl.ds(j, rows, stride=cuts), :] = answer[:, :lanes]
            wide_out[e][pl.ds(j + 1, rows, stride=cuts), :] = answer[:, lanes:]
        out_ref[:, e] = wide_out[e][...].astype(bf16).reshape(groups, capacity, cuts, lanes)


def combine_kernel(topk, slot_ref, weight_ref, back_ref, hidden_ref, out_ref, total):
    tokens, width = hidden_ref.shape
    cuts, lanes = back_ref.shape[1:]

    def add(t, carry):
        acc = jnp.zeros((cuts, lanes), f32)
        for k in range(topk):
            acc = acc + weight_ref[t, k] * back_ref[slot_ref[t * topk + k]].astype(f32)
        total[pl.ds(pl.multiple_of(t * cuts, cuts), cuts), :] = acc
        return carry

    lax.fori_loop(0, tokens, add, 0, unroll=2)
    for j in range(cuts):
        span = slice(j * lanes, (j + 1) * lanes)
        mixture = total[pl.ds(j, tokens, stride=cuts), :]
        out_ref[:, span] = (hidden_ref[:, span] + mixture).astype(bf16)


def shards(
    query_proj,
    key_proj,
    value_proj,
    output_gate,
    beta_logit,
    log_decay,
    norm_gain,
    out_weight,
    residual,
    moe_gain,
    expert_ids,
    route_weight,
    expert_gate,
    expert_up,
    expert_down,
):
    length, dk = query_proj.shape
    heads = beta_logit.shape[0]
    tokens, width = residual.shape
    experts_here, _, hidden_units = expert_gate.shape
    groups = lax.axis_size("ctx")
    topk = expert_ids.shape[1]
    capacity = 6
    lanes = 128
    cuts = width // lanes
    slots = groups * experts_here * capacity
    columns = 4
    pairs = lax.axis_size("exp") // 2
    rows = groups // columns
    along_x = [[y * columns + i for i in range(columns)] for y in range(rows)]
    along_y = [[y * columns + i for y in range(rows)] for i in range(columns)]
    half = dk * heads // columns

    def pair_swap(block):
        return lax.ppermute(block, "exp", [(i, i ^ 1) for i in range(2 * pairs)])

    def exchange(blocks, groups):
        return lax.all_to_all(blocks, "ctx", 0, 0, tiled=True, axis_index_groups=groups)

    other_weight = pair_swap(out_weight)

    slot, owner = pl.pallas_call(
        functools.partial(route_kernel, topk, capacity),
        out_shape=(
            jax.ShapeDtypeStruct((tokens * topk,), jnp.int32),
            jax.ShapeDtypeStruct((slots,), jnp.int32),
        ),
        in_specs=[smem()],
        out_specs=(smem(), smem()),
        scratch_shapes=[pltpu.SMEM((groups * experts_here,), jnp.int32)],
        name="route",
    )(expert_ids)

    carry, blend, own, packed = pl.pallas_call(
        functools.partial(scan_kernel, heads),
        out_shape=(
            jax.ShapeDtypeStruct((columns, heads, 2 * dk, dk), bf16),
            jax.ShapeDtypeStruct((heads, length, dk), bf16),
            jax.ShapeDtypeStruct((heads, length, dk), bf16),
            jax.ShapeDtypeStruct((2 * experts_here, lanes, hidden_units), bf16),
        ),
        in_specs=[vmem()] * 5 + [anywhere()] * 2,
        out_specs=(vmem(),) * 4,
        scratch_shapes=[pltpu.SemaphoreType.DMA((2,))],
        compiler_params=params(60),
        cost_estimate=cost(2e9, 4e6),
        name="scan",
    )(
        query_proj, key_proj, value_proj, beta_logit, log_decay,
        expert_gate, expert_up,
    )
    first_weights = lax.all_gather(packed, "exp", axis=0)

    maps = exchange(carry, along_x)
    totals, before = pl.pallas_call(
        row_kernel,
        out_shape=(
            jax.ShapeDtypeStruct((rows, dk + half, dk), bf16),
            jax.ShapeDtypeStruct((heads, 2 * dk, dk), bf16),
        ),
        in_specs=[vmem()],
        out_specs=(vmem(), vmem()),
        compiler_params=params(16),
        cost_estimate=cost(5e7, 1e6),
        name="row",
    )(maps)
    totals = exchange(totals, along_y)
    quarter = pl.pallas_call(
        column_kernel,
        out_shape=jax.ShapeDtypeStruct((columns, half, dk), bf16),
        in_specs=[vmem()],
        out_specs=vmem(),
        compiler_params=params(16),
        cost_estimate=cost(2e7, 5e5),
        name="column",
    )(totals)
    quarters = exchange(quarter, along_x)

    gated = pl.pallas_call(
        gate_kernel,
        out_shape=jax.ShapeDtypeStruct((2, pairs, tokens, heads * dk), bf16),
        in_specs=[vmem()] * 6,
        out_specs=vmem(),
        compiler_params=params(32),
        cost_estimate=cost(1e8, 2e6),
        name="gate",
    )(quarters, before, blend, own, output_gate, norm_gain.reshape(1, dk))
    got = pair_swap(gated[1])
    partial_sums = pl.pallas_call(
        project_kernel,
        out_shape=jax.ShapeDtypeStruct((pairs, tokens, width), bf16),
        in_specs=[vmem()] * 4,
        out_specs=vmem(),
        compiler_params=params(24),
        cost_estimate=cost(6e8, 4e6),
        name="project",
    )(gated, got, out_weight, other_weight)
    same_core = [[c + 2 * z for z in range(pairs)] for c in range(2)]
    parts = lax.all_to_all(
        partial_sums, "exp", 0, 0, tiled=True, axis_index_groups=same_core
    )

    hidden, outgoing, packed = pl.pallas_call(
        dispatch_kernel,
        out_shape=(
            jax.ShapeDtypeStruct((tokens, width), f32),
            jax.ShapeDtypeStruct((slots, cuts, lanes), bf16),
            jax.ShapeDtypeStruct((experts_here, lanes, hidden_units), bf16),
        ),
        in_specs=[smem(), vmem(), vmem(), vmem(), anywhere(), vmem()],
        out_specs=(vmem(), vmem(), anywhere()),
        scratch_shapes=[
            pltpu.VMEM((tokens * cuts, lanes), f32),
            pltpu.VMEM((tokens, cuts, lanes), bf16),
            pltpu.SemaphoreType.DMA((experts_here * (hidden_units // lanes),)),
        ],
        compiler_params=params(32),
        cost_estimate=cost(1e6, 3e6),
        name="dispatch",
    )(owner, parts, residual, moe_gain.reshape(1, width), expert_down, first_weights[0, 0, :16, :lanes])
    last_weights = lax.all_gather(packed, "exp", axis=0)
    outgoing = outgoing.reshape(groups, experts_here, capacity, cuts, lanes)
    incoming = lax.all_to_all(outgoing, "ctx", 0, 0, tiled=True)

    answers = pl.pallas_call(
        expert_kernel,
        out_shape=jax.ShapeDtypeStruct(incoming.shape, bf16),
        in_specs=[vmem(), anywhere(), anywhere()],
        out_specs=vmem(),
        scratch_shapes=[
            pltpu.VMEM(first_weights.shape, bf16),
            pltpu.VMEM(last_weights.shape, bf16),
            pltpu.SemaphoreType.DMA((3 * experts_here,)),
        ]
        + [pltpu.VMEM((groups * capacity * cuts, lanes), f32)] * (2 * experts_here)
        + [pltpu.VMEM((groups * capacity, width), bf16)] * experts_here,
        compiler_params=params(48),
        cost_estimate=cost(3e9, 16e6),
        name="experts",
    )(incoming, first_weights, last_weights)
    returned = lax.all_to_all(answers, "ctx", 0, 0, tiled=True).reshape(slots, cuts, lanes)

    return pl.pallas_call(
        functools.partial(combine_kernel, topk),
        out_shape=jax.ShapeDtypeStruct((tokens, width), bf16),
        in_specs=[smem(), smem(), vmem(), vmem()],
        out_specs=vmem(),
        scratch_shapes=[pltpu.VMEM((tokens * cuts, lanes), f32)],
        compiler_params=params(32),
        cost_estimate=cost(1e6, 3e6),
        name="combine",
    )(slot, route_weight, returned, hidden)


def solution(mesh):
    placed = (
        P("ctx", "exp"),
        P("ctx", "exp"),
        P("ctx", "exp"),
        P("ctx", "exp"),
        P("exp", "ctx"),
        P("exp", "ctx"),
        P(),
        P("exp", None),
        P(("ctx", "exp"), None),
        P(),
        P(("ctx", "exp"), None),
        P(("ctx", "exp"), None),
        P("ctx", "exp", None),
        P("ctx", "exp", None),
        P("ctx", None, "exp"),
    )
    return jax.shard_map(
        shards, mesh=mesh, in_specs=placed, out_specs=P(("ctx", "exp"), None), check_vma=False
    )
```

```python
import functools

import jax
import jax.numpy as jnp
from jax import lax
from jax.experimental import pallas as pl
from jax.experimental.pallas import tpu as pltpu
from jax.sharding import PartitionSpec as P

BLOCK = 128
f32 = jnp.float32
bf16 = jnp.bfloat16
VMEM = pltpu.VMEM
SMEM = pltpu.SMEM
MIB = 1 << 20


def vmem():
    return pl.BlockSpec(memory_space=VMEM)


def smem():
    return pl.BlockSpec(memory_space=SMEM)


def anywhere():
    return pl.BlockSpec(memory_space=pl.ANY)


def params(mib):
    return pltpu.CompilerParams(vmem_limit_bytes=mib * MIB)


def cost(flops, moved):
    return pl.CostEstimate(flops=int(flops), bytes_accessed=int(moved), transcendentals=0)


def mm(left, right):
    return jnp.dot(left.astype(bf16), right.astype(bf16), preferred_element_type=f32)


def mm_nt(left, right):
    return lax.dot_general(
        left.astype(bf16),
        right.astype(bf16),
        (((1,), (1,)), ((), ())),
        preferred_element_type=f32,
    )


def sigmoid(value):
    return 1.0 / (1.0 + jnp.exp(-value))


def start_copies(moves, sems):
    copies = [pltpu.make_async_copy(a, b, sems.at[i]) for i, (a, b) in enumerate(moves)]
    for copy in copies:
        copy.start()
    return copies


def pack_moves(gate_ref, up_ref, down_ref, early_ref, late_ref):
    experts, depth, lanes = down_ref.shape
    rows, split = early_ref.shape[1], early_ref.shape[0]
    halves = lanes // rows
    moves = []

    def add(source, place, *columns):
        home = early_ref.at[place] if place < split else late_ref.at[place - split]
        moves.append((source, home.at[(slice(None),) + columns] if columns else home))

    for e in range(experts):
        for i in range(halves):
            part = slice(i * rows, (i + 1) * rows)
            add(gate_ref.at[e, part], e * halves + i)
            add(up_ref.at[e, part], (experts + e) * halves + i)
            for b in range(0, depth, lanes):
                add(
                    down_ref.at[e, b + i * rows : b + (i + 1) * rows, :],
                    (2 * experts + e) * halves + i,
                    slice(b, b + lanes),
                )
    return moves


def scan_kernel(
    heads, q_ref, k_ref, v_ref, beta_ref, log_ref, output_gate_ref, gate_ref, up_ref, down_ref,
    carry_ref, kept_ref, sent_ref, early_ref, late_ref, sems,
):
    copies = start_copies(pack_moves(gate_ref, up_ref, down_ref, early_ref, late_ref), sems)
    length, dk = q_ref.shape
    count = length // BLOCK
    tokens = kept_ref.shape[2]
    first_core = lax.rem(lax.axis_index("exp"), 2) == 0

    def put(part, c, lanes, value):
        for b in range(0, BLOCK, 2 * tokens):
            pair = (c * BLOCK + b) // (2 * tokens)
            even, odd = value[b : b + tokens], value[b + tokens : b + 2 * tokens]
            kept_ref[part, pair, :, lanes] = jnp.where(first_core, even, odd)
            sent_ref[part, pair, :, lanes] = jnp.where(first_core, odd, even)

    row = lax.broadcasted_iota(jnp.int32, (BLOCK, BLOCK), 0)
    col = lax.broadcasted_iota(jnp.int32, (BLOCK, BLOCK), 1)
    problems = []
    for c in range(count):
        span = slice(c * BLOCK, (c + 1) * BLOCK)
        keys, queries = k_ref[span, :], q_ref[span, :]
        key_values, query_values = keys.astype(f32), queries.astype(f32)
        key_scale = lax.rsqrt(jnp.sum(key_values * key_values, 1, keepdims=True) + 1e-06)
        query_scale = lax.rsqrt(
            jnp.sum(query_values * query_values, 1, keepdims=True) + 1e-06
        ) * dk ** (-0.5)
        key_scale_row = jnp.sum(jnp.where(row == col, key_scale, 0.0), 0, keepdims=True)
        key_key = mm_nt(keys, keys) * key_scale * key_scale_row
        query_key = mm_nt(queries, keys) * query_scale * key_scale_row
        keys_t = jnp.transpose(key_values)
        for h in range(heads):
            logs = log_ref[h : h + 1, span]
            beta = sigmoid(beta_ref[h : h + 1, span])
            logs_col = jnp.sum(jnp.where(row == col, logs, 0.0), 1, keepdims=True)
            total_row = jnp.sum(jnp.where(row <= col, logs_col, 0.0), 0, keepdims=True)
            total_col = jnp.sum(jnp.where(col <= row, logs, 0.0), 1, keepdims=True)
            within = row >= col
            mask = jnp.where(
                within, jnp.exp(jnp.where(within, total_col - total_row, 0.0)), 0.0
            ) * beta
            lower = jnp.where(row > col, key_key * mask, 0.0)
            end = total_row[:, BLOCK - 1 : BLOCK]
            problems.append(
                dict(
                    lower=lower,
                    inverse=jnp.where(row == col, 1.0, 0.0)
                    - jnp.where(row // 2 == col // 2, lower, 0.0),
                    scores=(query_key * mask).astype(bf16),
                    into=jnp.exp(total_row) * key_scale_row,
                    queries=query_values * (jnp.exp(total_col) * query_scale),
                    tail=(keys_t * (jnp.exp(end - total_row) * beta * key_scale_row)).astype(bf16),
                    gain=jnp.exp(end),
                    keys=keys,
                    values=v_ref[span, h * dk : (h + 1) * dk],
                )
            )
    width = 2
    while width < BLOCK:
        pick = (row // (2 * width) == col // (2 * width)) & (row // width != col // width)
        for p in problems:
            inverse = p["inverse"].astype(bf16)
            step = mm(inverse, jnp.where(pick, p["lower"], 0.0))
            p["inverse"] = p["inverse"] - mm(step, inverse)
        width *= 2
    for p in problems:
        p["both"] = jnp.concatenate(
            [mm(p["inverse"] * p["into"], p["keys"]), mm(p["inverse"], p["values"])], 1
        ).astype(bf16)
    for p in problems:
        p["seen"] = mm(p["scores"], p["both"])
        p["push"] = mm(p["tail"], p["both"])
    states = []
    for h in range(heads):
        states.append(
            jnp.concatenate(
                [jnp.where(row == col, 1.0, 0.0), jnp.zeros((dk, dk), f32)], 1
            )
        )
    for c in range(count):
        span = slice(c * BLOCK, (c + 1) * BLOCK)
        for h in range(heads):
            p = problems[c * heads + h]
            state = states[h]
            low = state.astype(bf16)
            out = mm(p["queries"] - p["seen"][:, :dk], low)
            lanes = slice(h * dk, (h + 1) * dk)
            put(0, c, lanes, out[:, :dk].astype(bf16))
            put(1, c, lanes, (out[:, dk:] + p["seen"][:, dk:]).astype(bf16))
            put(2, c, lanes, output_gate_ref[span, lanes])
            push = p["push"]
            moved = mm(push[:, :dk], low)
            states[h] = jnp.concatenate(
                [
                    p["gain"] * state[:, :dk] - moved[:, :dk],
                    p["gain"] * state[:, dk:] - moved[:, dk:] + push[:, dk:],
                ],
                1,
            )
    for h in range(heads):
        for part in range(2):
            turned = jnp.transpose(states[h][:, part * dk : (part + 1) * dk]).astype(bf16)
            for place in range(carry_ref.shape[0]):
                carry_ref[place, h, part * dk : (part + 1) * dk, :] = turned
    for copy in copies:
        copy.wait()


def follow(late, early):
    dk = late.shape[-1]
    moved = mm(early, late[:dk])
    return jnp.concatenate([moved[:dk], moved[dk:] + late[dk:].astype(f32)], 0).astype(bf16)


def row_kernel(maps_ref, total_ref, before_ref):
    columns, heads, _, dk = maps_ref.shape
    x = lax.rem(lax.axis_index("ctx"), columns)
    half = dk * heads // columns
    for place in range(columns):

        @pl.when(x == place)
        def _():
            for h in range(heads):
                parts = [maps_ref[j, h] for j in range(columns)]
                prefix = parts[0]
                for j in range(1, place):
                    prefix = follow(parts[j], prefix)
                if place == 0:
                    eye = lax.broadcasted_iota(jnp.int32, (dk, dk), 0) == (
                        lax.broadcasted_iota(jnp.int32, (dk, dk), 1)
                    )
                    prefix = jnp.concatenate(
                        [jnp.where(eye, 1.0, 0.0), jnp.zeros((dk, dk), f32)], 0
                    ).astype(bf16)
                before_ref[h] = prefix
                if h == place * heads // columns:
                    low = dk + (place % (columns // heads)) * half
                    cut = [
                        jnp.concatenate([part[:dk], part[low : low + half]], 0) for part in parts
                    ]
                    total = cut[0]
                    for j in range(1, columns):
                        total = follow(cut[j], total)
                    for row in range(total_ref.shape[0]):
                        total_ref[row] = total


def column_kernel(totals_ref, out_ref):
    dk = totals_ref.shape[2]
    y = lax.axis_index("ctx") // (out_ref.shape[0] // 2)

    state = jnp.zeros(out_ref.shape[1:], f32)
    for j in range(totals_ref.shape[0] - 1):
        moved = mm(state, totals_ref[j, :dk, :]) + totals_ref[j, dk:, :].astype(f32)
        state = jnp.where(j < y, moved, state)
    state = state.astype(bf16)
    for place in range(out_ref.shape[0]):
        out_ref[place] = state


def project_kernel(
    quarters_ref, before_ref, other_before_ref, kept_ref, got_ref, gain_ref, weight_ref,
    other_weight_ref, out_ref,
):
    core = lax.rem(lax.axis_index("exp"), 2)
    heads, _, dk = before_ref.shape
    _, pairs, tokens, _ = kept_ref.shape
    rows = pairs * tokens
    columns = quarters_ref.shape[0] // 2
    share = columns // heads
    gain = gain_ref[...]
    total = 0.0
    for source, before, base, weight in (
        (kept_ref, before_ref, core * columns, weight_ref),
        (got_ref, other_before_ref, (1 - core) * columns, other_weight_ref),
    ):
        gated = []
        for h in range(heads):
            lanes = slice(h * dk, (h + 1) * dk)
            row_state = jnp.concatenate(
                [quarters_ref[base + share * h + i] for i in range(share)], 0
            )
            entry = mm(row_state, before[h, :dk, :]) + before[h, dk:, :].astype(f32)
            mixed = mm_nt(source[0, :, :, lanes].reshape(rows, dk), entry)
            mixed = mixed + source[1, :, :, lanes].astype(f32).reshape(rows, dk)
            scale = lax.rsqrt(jnp.mean(mixed * mixed, 1, keepdims=True) + 1e-06)
            gates = source[2, :, :, lanes].astype(f32).reshape(rows, dk)
            gated.append((mixed * scale * gain * (gates * sigmoid(gates))).astype(bf16))
        total = total + mm(jnp.concatenate(gated, 1), weight[...])
    out_ref[...] = total.astype(bf16).reshape(out_ref.shape)


def route_kernel(topk, capacity, ids_ref, slot_ref, owner_ref, count_ref):
    tokens = ids_ref.shape[0]
    experts = count_ref.shape[0]

    def clear(i, carry):
        count_ref[i] = 0
        for r in range(capacity):
            owner_ref[i * capacity + r] = 0
        return carry

    lax.fori_loop(0, experts, clear, 0)

    def place(t, carry):
        for k in range(topk):
            expert = ids_ref[t, k]
            rank = count_ref[expert]
            count_ref[expert] = rank + 1
            slot = expert * capacity + rank
            slot_ref[t * topk + k] = slot
            owner_ref[slot] = t
        return carry

    lax.fori_loop(0, tokens, place, 0)


def dispatch_kernel(
    owner_ref, parts_ref, residual_ref, gain_ref, after_ref, late_ref,
    hidden_ref, out_ref, same_late_ref, rows_ref, tiles_ref,
):
    sources, tokens, width = parts_ref.shape
    lanes = out_ref.shape[2]
    cuts = width // lanes
    hidden = parts_ref[0].astype(f32)
    for s in range(1, sources):
        hidden = hidden + parts_ref[s].astype(f32)
    hidden = hidden + residual_ref[...].astype(f32)
    hidden_ref[...] = hidden
    scale = lax.rsqrt(jnp.mean(hidden * hidden, 1, keepdims=True) + 1e-06)
    normed = hidden * scale * gain_ref[...]
    for j in range(cuts):
        rows_ref[pl.ds(j, tokens, stride=cuts), :] = normed[:, j * lanes : (j + 1) * lanes]
    tiles_ref[...] = rows_ref[...].astype(bf16).reshape(tiles_ref.shape)
    unroll = 8

    def place(i, carry):
        for u in range(unroll):
            slot = i * unroll + u
            out_ref[slot] = tiles_ref[owner_ref[slot]]
        return carry

    lax.fori_loop(0, out_ref.shape[0] // unroll, place, 0)


def expert_kernel(rows_ref, early_ref, late_ref, out_ref, weights, sems, *scratch):
    groups, experts, capacity, cuts, lanes = rows_ref.shape
    split, height = early_ref.shape[1:3]
    halves = lanes // height
    order = [
        (m * experts + e) * halves + i for e in range(experts) for m in range(3) for i in range(halves)
    ]
    copies = start_copies(
        [
            (
                early_ref.at[:, m] if m < split else late_ref.at[:, m - split],
                weights.at[:, m],
            )
            for m in order
        ],
        sems,
    )

    def matrix(e, m):
        for i in range(halves):
            copies[(3 * e + m) * halves + i].wait()
        return slice((m * experts + e) * halves, (m * experts + e + 1) * halves)

    rows = groups * capacity
    hidden_units = early_ref.shape[3]
    depth = cuts * lanes
    wide_in, wide_out, flat = scratch[:experts], scratch[experts : 2 * experts], scratch[2 * experts :]
    for e in range(experts):
        wide_in[e][...] = rows_ref[:, e].astype(f32).reshape(rows * cuts, lanes)
        for j in range(cuts):
            part = wide_in[e][pl.ds(j, rows, stride=cuts), :]
            flat[e][:, j * lanes : (j + 1) * lanes] = part.astype(bf16)
    for e in range(experts):
        tokens = flat[e][...]
        first = mm(tokens, weights[:, matrix(e, 0)].reshape(depth, hidden_units))
        second = mm(tokens, weights[:, matrix(e, 1)].reshape(depth, hidden_units))
        inner = (first * sigmoid(first) * second).astype(bf16)
        last = matrix(e, 2)
        for j in range(0, cuts, 2):
            columns = []
            for k in (j, j + 1):
                columns.append(
                    jnp.concatenate(
                        [
                            weights[k, last, :, b : b + lanes].reshape(lanes, lanes)
                            for b in range(0, hidden_units, lanes)
                        ],
                        0,
                    )
                )
            answer = mm(inner, jnp.concatenate(columns, 1))
            wide_out[e][pl.ds(j, rows, stride=cuts), :] = answer[:, :lanes]
            wide_out[e][pl.ds(j + 1, rows, stride=cuts), :] = answer[:, lanes:]
        out_ref[:, e] = wide_out[e][...].astype(bf16).reshape(groups, capacity, cuts, lanes)


def combine_kernel(topk, slot_ref, weight_ref, back_ref, hidden_ref, out_ref, total):
    tokens, width = hidden_ref.shape
    cuts, lanes = back_ref.shape[1:]

    def add(t, carry):
        acc = jnp.zeros((cuts, lanes), f32)
        for k in range(topk):
            acc = acc + weight_ref[t, k] * back_ref[slot_ref[t * topk + k]].astype(f32)
        total[pl.ds(pl.multiple_of(t * cuts, cuts), cuts), :] = acc
        return carry

    lax.fori_loop(0, tokens, add, 0, unroll=2)
    for j in range(cuts):
        span = slice(j * lanes, (j + 1) * lanes)
        mixture = total[pl.ds(j, tokens, stride=cuts), :]
        out_ref[:, span] = (hidden_ref[:, span] + mixture).astype(bf16)


def shards(
    query_proj,
    key_proj,
    value_proj,
    output_gate,
    beta_logit,
    log_decay,
    norm_gain,
    out_weight,
    residual,
    moe_gain,
    expert_ids,
    route_weight,
    expert_gate,
    expert_up,
    expert_down,
):
    length, dk = query_proj.shape
    heads = beta_logit.shape[0]
    tokens, width = residual.shape
    experts_here, _, hidden_units = expert_gate.shape
    groups = lax.axis_size("ctx")
    topk = expert_ids.shape[1]
    capacity = 6
    lanes = 128
    cuts = width // lanes
    slots = groups * experts_here * capacity
    columns = 4
    pairs = lax.axis_size("exp") // 2
    rows = groups // columns
    along_x = [[y * columns + i for i in range(columns)] for y in range(rows)]
    along_y = [[y * columns + i for y in range(rows)] for i in range(columns)]
    half = dk * heads // columns

    def pair_swap(block):
        return lax.ppermute(block, "exp", [(i, i ^ 1) for i in range(2 * pairs)])

    def exchange(blocks, groups):
        return lax.all_to_all(blocks, "ctx", 0, 0, tiled=True, axis_index_groups=groups)

    other_weight = pair_swap(out_weight)

    slot, owner = pl.pallas_call(
        functools.partial(route_kernel, topk, capacity),
        out_shape=(
            jax.ShapeDtypeStruct((tokens * topk,), jnp.int32),
            jax.ShapeDtypeStruct((slots,), jnp.int32),
        ),
        in_specs=[smem()],
        out_specs=(smem(), smem()),
        scratch_shapes=[pltpu.SMEM((groups * experts_here,), jnp.int32)],
        name="route",
    )(expert_ids)

    early_halves = 7
    package = jax.ShapeDtypeStruct((3, pairs, tokens, heads * dk), bf16)
    carry, kept, sent, early, late = pl.pallas_call(
        functools.partial(scan_kernel, heads),
        out_shape=(
            jax.ShapeDtypeStruct((columns, heads, 2 * dk, dk), bf16),
            package,
            package,
            jax.ShapeDtypeStruct((early_halves, lanes // 2, hidden_units), bf16),
            jax.ShapeDtypeStruct((6 * experts_here - early_halves, lanes // 2, hidden_units), bf16),
        ),
        in_specs=[vmem()] * 6 + [anywhere()] * 3,
        out_specs=(vmem(),) * 5,
        scratch_shapes=[
            pltpu.SemaphoreType.DMA((2 * experts_here * (2 + hidden_units // lanes),))
        ],
        compiler_params=params(60),
        cost_estimate=cost(2e9, 4e6),
        name="scan",
    )(
        query_proj, key_proj, value_proj, beta_logit, log_decay, output_gate,
        expert_gate, expert_up, expert_down,
    )
    got = pair_swap(sent)
    early = lax.all_gather(early, "exp", axis=0)

    maps = exchange(carry, along_x)
    totals, before = pl.pallas_call(
        row_kernel,
        out_shape=(
            jax.ShapeDtypeStruct((rows, dk + half, dk), bf16),
            jax.ShapeDtypeStruct((heads, 2 * dk, dk), bf16),
        ),
        in_specs=[vmem()],
        out_specs=(vmem(), vmem()),
        compiler_params=params(16),
        cost_estimate=cost(5e7, 1e6),
        name="row",
    )(maps)
    other_before = pair_swap(before)
    totals = exchange(totals, along_y)
    quarter = pl.pallas_call(
        column_kernel,
        out_shape=jax.ShapeDtypeStruct((2 * columns, half, dk), bf16),
        in_specs=[vmem()],
        out_specs=vmem(),
        compiler_params=params(16),
        cost_estimate=cost(2e7, 5e5),
        name="column",
    )(totals)
    quarters = lax.all_to_all(
        quarter,
        ("ctx", "exp"),
        0,
        0,
        tiled=True,
        axis_index_groups=[
            [(y * columns + x) * 2 * pairs + 2 * z + c for c in range(2) for x in range(columns)]
            for y in range(rows)
            for z in range(pairs)
        ],
    )

    partial_sums = pl.pallas_call(
        project_kernel,
        out_shape=jax.ShapeDtypeStruct((pairs, tokens, width), bf16),
        in_specs=[vmem()] * 8,
        out_specs=vmem(),
        compiler_params=params(24),
        cost_estimate=cost(6e8, 4e6),
        name="project",
    )(
        quarters, before, other_before, kept, got, norm_gain.reshape(1, dk),
        out_weight, other_weight,
    )
    same_core = [[c + 2 * z for z in range(pairs)] for c in range(2)]
    parts = lax.all_to_all(
        partial_sums, "exp", 0, 0, tiled=True, axis_index_groups=same_core
    )

    hidden, outgoing, late = pl.pallas_call(
        dispatch_kernel,
        out_shape=(
            jax.ShapeDtypeStruct((tokens, width), f32),
            jax.ShapeDtypeStruct((slots, cuts, lanes), bf16),
            jax.ShapeDtypeStruct(late.shape, bf16),
        ),
        in_specs=[smem(), vmem(), vmem(), vmem(), vmem(), anywhere()],
        out_specs=(vmem(), vmem(), anywhere()),
        input_output_aliases={5: 2},
        scratch_shapes=[
            pltpu.VMEM((tokens * cuts, lanes), f32),
            pltpu.VMEM((tokens, cuts, lanes), bf16),
        ],
        compiler_params=params(32),
        cost_estimate=cost(1e6, 3e6),
        name="dispatch",
    )(owner, parts, residual, moe_gain.reshape(1, width), early[0, 0, :16, :lanes], late)
    late = lax.all_gather(late, "exp", axis=0)
    outgoing = outgoing.reshape(groups, experts_here, capacity, cuts, lanes)
    incoming = lax.all_to_all(outgoing, "ctx", 0, 0, tiled=True)

    answers = pl.pallas_call(
        expert_kernel,
        out_shape=jax.ShapeDtypeStruct(incoming.shape, bf16),
        in_specs=[vmem(), anywhere(), anywhere()],
        out_specs=vmem(),
        scratch_shapes=[
            pltpu.VMEM((2 * pairs, 6 * experts_here, lanes // 2, hidden_units), bf16),
            pltpu.SemaphoreType.DMA((6 * experts_here,)),
        ]
        + [pltpu.VMEM((groups * capacity * cuts, lanes), f32)] * (2 * experts_here)
        + [pltpu.VMEM((groups * capacity, width), bf16)] * experts_here,
        compiler_params=params(48),
        cost_estimate=cost(3e9, 16e6),
        name="experts",
    )(incoming, early, late)
    returned = lax.all_to_all(answers, "ctx", 0, 0, tiled=True).reshape(slots, cuts, lanes)

    return pl.pallas_call(
        functools.partial(combine_kernel, topk),
        out_shape=jax.ShapeDtypeStruct((tokens, width), bf16),
        in_specs=[smem(), smem(), vmem(), vmem()],
        out_specs=vmem(),
        scratch_shapes=[pltpu.VMEM((tokens * cuts, lanes), f32)],
        compiler_params=params(32),
        cost_estimate=cost(1e6, 3e6),
        name="combine",
    )(slot, route_weight, returned, hidden)


def solution(mesh):
    placed = (
        P("ctx", "exp"),
        P("ctx", "exp"),
        P("ctx", "exp"),
        P("ctx", "exp"),
        P("exp", "ctx"),
        P("exp", "ctx"),
        P(),
        P("exp", None),
        P(("ctx", "exp"), None),
        P(),
        P(("ctx", "exp"), None),
        P(("ctx", "exp"), None),
        P("ctx", "exp", None),
        P("ctx", "exp", None),
        P("ctx", None, "exp"),
    )
    return jax.shard_map(
        shards, mesh=mesh, in_specs=placed, out_specs=P(("ctx", "exp"), None), check_vma=False
    )
```

```python
import functools

import jax
import jax.numpy as jnp
from jax import lax
from jax.experimental import pallas as pl
from jax.experimental.pallas import tpu as pltpu
from jax.sharding import PartitionSpec as P

BLOCK = 128
f32 = jnp.float32
bf16 = jnp.bfloat16
VMEM = pltpu.VMEM
SMEM = pltpu.SMEM
MIB = 1 << 20


def vmem():
    return pl.BlockSpec(memory_space=VMEM)


def smem():
    return pl.BlockSpec(memory_space=SMEM)


def anywhere():
    return pl.BlockSpec(memory_space=pl.ANY)


def params(mib):
    return pltpu.CompilerParams(vmem_limit_bytes=mib * MIB)


def cost(flops, moved):
    return pl.CostEstimate(flops=int(flops), bytes_accessed=int(moved), transcendentals=0)


def mm(left, right):
    return jnp.dot(left.astype(bf16), right.astype(bf16), preferred_element_type=f32)


def mm_nt(left, right):
    return lax.dot_general(
        left.astype(bf16),
        right.astype(bf16),
        (((1,), (1,)), ((), ())),
        preferred_element_type=f32,
    )


def sigmoid(value):
    return 1.0 / (1.0 + jnp.exp(-value))


def start_copies(moves, sems):
    copies = [pltpu.make_async_copy(a, b, sems.at[i]) for i, (a, b) in enumerate(moves)]
    for copy in copies:
        copy.start()
    return copies


def pack_moves(gate_ref, up_ref, down_ref, early_ref, late_ref):
    experts, depth, lanes = down_ref.shape
    rows, split = early_ref.shape[1], early_ref.shape[0]
    halves = lanes // rows
    moves = []

    def add(source, place, *columns):
        home = early_ref.at[place] if place < split else late_ref.at[place - split]
        moves.append((source, home.at[(slice(None),) + columns] if columns else home))

    for e in range(experts):
        for i in range(halves):
            part = slice(i * rows, (i + 1) * rows)
            add(gate_ref.at[e, part], e * halves + i)
            add(up_ref.at[e, part], (experts + e) * halves + i)
            for b in range(0, depth, lanes):
                add(
                    down_ref.at[e, b + i * rows : b + (i + 1) * rows, :],
                    (2 * experts + e) * halves + i,
                    slice(b, b + lanes),
                )
    return moves


def scan_kernel(
    heads, q_ref, k_ref, v_ref, beta_ref, log_ref, output_gate_ref, gate_ref, up_ref, down_ref,
    carry_ref, kept_ref, sent_ref, early_ref, late_ref, sems,
):
    copies = start_copies(pack_moves(gate_ref, up_ref, down_ref, early_ref, late_ref), sems)
    length, dk = q_ref.shape
    count = length // BLOCK
    tokens = kept_ref.shape[2]
    first_core = lax.rem(lax.axis_index("exp"), 2) == 0

    def put(part, c, lanes, value):
        for b in range(0, BLOCK, 2 * tokens):
            pair = (c * BLOCK + b) // (2 * tokens)
            even, odd = value[b : b + tokens], value[b + tokens : b + 2 * tokens]
            kept_ref[part, pair, :, lanes] = jnp.where(first_core, even, odd)
            sent_ref[part, pair, :, lanes] = jnp.where(first_core, odd, even)

    row = lax.broadcasted_iota(jnp.int32, (BLOCK, BLOCK), 0)
    col = lax.broadcasted_iota(jnp.int32, (BLOCK, BLOCK), 1)
    problems = []
    for c in range(count):
        span = slice(c * BLOCK, (c + 1) * BLOCK)
        keys, queries = k_ref[span, :], q_ref[span, :]
        key_values, query_values = keys.astype(f32), queries.astype(f32)
        key_scale = lax.rsqrt(jnp.sum(key_values * key_values, 1, keepdims=True) + 1e-06)
        query_scale = lax.rsqrt(
            jnp.sum(query_values * query_values, 1, keepdims=True) + 1e-06
        ) * dk ** (-0.5)
        key_scale_row = jnp.sum(jnp.where(row == col, key_scale, 0.0), 0, keepdims=True)
        key_key = mm_nt(keys, keys) * key_scale * key_scale_row
        query_key = mm_nt(queries, keys) * query_scale * key_scale_row
        keys_t = jnp.transpose(key_values)
        for h in range(heads):
            logs = log_ref[h : h + 1, span]
            beta = sigmoid(beta_ref[h : h + 1, span])
            logs_col = jnp.sum(jnp.where(row == col, logs, 0.0), 1, keepdims=True)
            total_row = jnp.sum(jnp.where(row <= col, logs_col, 0.0), 0, keepdims=True)
            total_col = jnp.sum(jnp.where(col <= row, logs, 0.0), 1, keepdims=True)
            within = row >= col
            mask = jnp.where(
                within, jnp.exp(jnp.where(within, total_col - total_row, 0.0)), 0.0
            ) * beta
            lower = jnp.where(row > col, key_key * mask, 0.0)
            end = total_row[:, BLOCK - 1 : BLOCK]
            problems.append(
                dict(
                    lower=lower,
                    inverse=jnp.where(row == col, 1.0, 0.0)
                    - jnp.where(row // 2 == col // 2, lower, 0.0),
                    scores=(query_key * mask).astype(bf16),
                    into=jnp.exp(total_row) * key_scale_row,
                    queries=query_values * (jnp.exp(total_col) * query_scale),
                    tail=(keys_t * (jnp.exp(end - total_row) * beta * key_scale_row)).astype(bf16),
                    gain=jnp.exp(end),
                    keys=keys,
                    values=v_ref[span, h * dk : (h + 1) * dk],
                )
            )
    width = 2
    while width < BLOCK:
        pick = (row // (2 * width) == col // (2 * width)) & (row // width != col // width)
        for p in problems:
            inverse = p["inverse"].astype(bf16)
            step = mm(inverse, jnp.where(pick, p["lower"], 0.0))
            p["inverse"] = p["inverse"] - mm(step, inverse)
        width *= 2
    for p in problems:
        p["both"] = jnp.concatenate(
            [mm(p["inverse"] * p["into"], p["keys"]), mm(p["inverse"], p["values"])], 1
        ).astype(bf16)
    for p in problems:
        p["seen"] = mm(p["scores"], p["both"])
        p["push"] = mm(p["tail"], p["both"])
    states = []
    for h in range(heads):
        states.append(
            jnp.concatenate(
                [jnp.where(row == col, 1.0, 0.0), jnp.zeros((dk, dk), f32)], 1
            )
        )
    for c in range(count):
        span = slice(c * BLOCK, (c + 1) * BLOCK)
        for h in range(heads):
            p = problems[c * heads + h]
            state = states[h]
            low = state.astype(bf16)
            out = mm(p["queries"] - p["seen"][:, :dk], low)
            lanes = slice(h * dk, (h + 1) * dk)
            put(0, c, lanes, out[:, :dk].astype(bf16))
            put(1, c, lanes, (out[:, dk:] + p["seen"][:, dk:]).astype(bf16))
            put(2, c, lanes, output_gate_ref[span, lanes])
            push = p["push"]
            moved = mm(push[:, :dk], low)
            states[h] = jnp.concatenate(
                [
                    p["gain"] * state[:, :dk] - moved[:, :dk],
                    p["gain"] * state[:, dk:] - moved[:, dk:] + push[:, dk:],
                ],
                1,
            )
    for h in range(heads):
        for part in range(2):
            turned = jnp.transpose(states[h][:, part * dk : (part + 1) * dk]).astype(bf16)
            for place in range(carry_ref.shape[0]):
                carry_ref[place, h, part * dk : (part + 1) * dk, :] = turned
    for copy in copies:
        copy.wait()


def follow(late, early):
    dk = late.shape[-1]
    moved = mm(early, late[:dk])
    return jnp.concatenate([moved[:dk], moved[dk:] + late[dk:].astype(f32)], 0).astype(bf16)


def row_kernel(maps_ref, total_ref, before_ref):
    columns, heads, _, dk = maps_ref.shape
    x = lax.rem(lax.axis_index("ctx"), columns)
    half = dk * heads // columns
    for place in range(columns):

        @pl.when(x == place)
        def _():
            for h in range(heads):
                parts = [maps_ref[j, h] for j in range(columns)]
                prefix = parts[0]
                for j in range(1, place):
                    prefix = follow(parts[j], prefix)
                if place == 0:
                    eye = lax.broadcasted_iota(jnp.int32, (dk, dk), 0) == (
                        lax.broadcasted_iota(jnp.int32, (dk, dk), 1)
                    )
                    prefix = jnp.concatenate(
                        [jnp.where(eye, 1.0, 0.0), jnp.zeros((dk, dk), f32)], 0
                    ).astype(bf16)
                before_ref[h] = prefix
                if h == place * heads // columns:
                    low = dk + (place % (columns // heads)) * half
                    cut = [
                        jnp.concatenate([part[:dk], part[low : low + half]], 0) for part in parts
                    ]
                    total = cut[0]
                    for j in range(1, columns):
                        total = follow(cut[j], total)
                    for row in range(total_ref.shape[0]):
                        total_ref[row] = total


def column_kernel(totals_ref, out_ref):
    dk = totals_ref.shape[2]
    y = lax.axis_index("ctx") // (out_ref.shape[0] // 2)

    state = jnp.zeros(out_ref.shape[1:], f32)
    for j in range(totals_ref.shape[0] - 1):
        moved = mm(state, totals_ref[j, :dk, :]) + totals_ref[j, dk:, :].astype(f32)
        state = jnp.where(j < y, moved, state)
    state = state.astype(bf16)
    for place in range(out_ref.shape[0]):
        out_ref[place] = state


def project_kernel(
    quarters_ref, before_ref, other_before_ref, kept_ref, got_ref, gain_ref, weight_ref,
    other_weight_ref, out_ref,
):
    core = lax.rem(lax.axis_index("exp"), 2)
    heads, _, dk = before_ref.shape
    _, pairs, tokens, _ = kept_ref.shape
    rows = pairs * tokens
    columns = quarters_ref.shape[0] // 2
    share = columns // heads
    gain = gain_ref[...]
    total = 0.0
    for source, before, base, weight in (
        (kept_ref, before_ref, core * columns, weight_ref),
        (got_ref, other_before_ref, (1 - core) * columns, other_weight_ref),
    ):
        gated = []
        for h in range(heads):
            lanes = slice(h * dk, (h + 1) * dk)
            row_state = jnp.concatenate(
                [quarters_ref[base + share * h + i] for i in range(share)], 0
            )
            entry = mm(row_state, before[h, :dk, :]) + before[h, dk:, :].astype(f32)
            mixed = mm_nt(source[0, :, :, lanes].reshape(rows, dk), entry)
            mixed = mixed + source[1, :, :, lanes].astype(f32).reshape(rows, dk)
            scale = lax.rsqrt(jnp.mean(mixed * mixed, 1, keepdims=True) + 1e-06)
            gates = source[2, :, :, lanes].astype(f32).reshape(rows, dk)
            gated.append((mixed * scale * gain * (gates * sigmoid(gates))).astype(bf16))
        total = total + mm(jnp.concatenate(gated, 1), weight[...])
    out_ref[...] = total.astype(bf16).reshape(out_ref.shape)


def route_kernel(topk, capacity, ids_ref, slot_ref, owner_ref, count_ref):
    tokens = ids_ref.shape[0]
    experts = count_ref.shape[0]

    def clear(i, carry):
        count_ref[i] = 0
        for r in range(capacity):
            owner_ref[i * capacity + r] = 0
        return carry

    lax.fori_loop(0, experts, clear, 0)

    def place(t, carry):
        for k in range(topk):
            expert = ids_ref[t, k]
            rank = count_ref[expert]
            count_ref[expert] = rank + 1
            slot = expert * capacity + rank
            slot_ref[t * topk + k] = slot
            owner_ref[slot] = t
        return carry

    lax.fori_loop(0, tokens, place, 0)


def dispatch_kernel(
    owner_ref, parts_ref, residual_ref, gain_ref, after_ref, late_ref,
    hidden_ref, out_ref, same_late_ref, rows_ref, tiles_ref,
):
    sources, tokens, width = parts_ref.shape
    lanes = out_ref.shape[2]
    cuts = width // lanes
    hidden = parts_ref[0].astype(f32)
    for s in range(1, sources):
        hidden = hidden + parts_ref[s].astype(f32)
    hidden = hidden + residual_ref[...].astype(f32)
    hidden_ref[...] = hidden
    scale = lax.rsqrt(jnp.mean(hidden * hidden, 1, keepdims=True) + 1e-06)
    normed = hidden * scale * gain_ref[...]
    for j in range(cuts):
        rows_ref[pl.ds(j, tokens, stride=cuts), :] = normed[:, j * lanes : (j + 1) * lanes]
    tiles_ref[...] = rows_ref[...].astype(bf16).reshape(tiles_ref.shape)
    unroll = 8

    def place(i, carry):
        for u in range(unroll):
            slot = i * unroll + u
            out_ref[slot] = tiles_ref[owner_ref[slot]]
        return carry

    lax.fori_loop(0, out_ref.shape[0] // unroll, place, 0)


def expert_kernel(rows_ref, early_ref, late_ref, out_ref, weights, ready, sems, out_sems, *scratch):
    groups, experts, capacity, cuts, lanes = rows_ref.shape
    split, height = early_ref.shape[1:3]
    halves = lanes // height
    order = [
        (m * experts + e) * halves + i for e in range(experts) for m in range(3) for i in range(halves)
    ]
    copies = start_copies(
        [
            (
                early_ref.at[:, m] if m < split else late_ref.at[:, m - split],
                weights.at[:, m],
            )
            for m in order
        ],
        sems,
    )

    def matrix(e, m):
        for i in range(halves):
            copies[(3 * e + m) * halves + i].wait()
        return slice((m * experts + e) * halves, (m * experts + e + 1) * halves)

    rows = groups * capacity
    hidden_units = early_ref.shape[3]
    depth = cuts * lanes
    wide_in, wide_out, flat = scratch[:experts], scratch[experts : 2 * experts], scratch[2 * experts :]
    sent = []
    for e in range(experts):
        wide_in[e][...] = rows_ref[:, e].astype(f32).reshape(rows * cuts, lanes)
        for j in range(cuts):
            part = wide_in[e][pl.ds(j, rows, stride=cuts), :]
            flat[e][:, j * lanes : (j + 1) * lanes] = part.astype(bf16)
    for e in range(experts):
        tokens = flat[e][...]
        first = mm(tokens, weights[:, matrix(e, 0)].reshape(depth, hidden_units))
        second = mm(tokens, weights[:, matrix(e, 1)].reshape(depth, hidden_units))
        inner = (first * sigmoid(first) * second).astype(bf16)
        last = matrix(e, 2)
        for j in range(0, cuts, 2):
            columns = []
            for k in (j, j + 1):
                columns.append(
                    jnp.concatenate(
                        [
                            weights[k, last, :, b : b + lanes].reshape(lanes, lanes)
                            for b in range(0, hidden_units, lanes)
                        ],
                        0,
                    )
                )
            answer = mm(inner, jnp.concatenate(columns, 1))
            wide_out[e][pl.ds(j, rows, stride=cuts), :] = answer[:, :lanes]
            wide_out[e][pl.ds(j + 1, rows, stride=cuts), :] = answer[:, lanes:]
        ready[e] = wide_out[e][...].astype(bf16).reshape(groups, capacity, cuts, lanes)
        sent.append(pltpu.make_async_copy(ready.at[e], out_ref.at[:, e], out_sems.at[e]))
        sent[e].start()
    for copy in sent:
        copy.wait()


def combine_kernel(topk, slot_ref, weight_ref, back_ref, hidden_ref, out_ref, total):
    tokens, width = hidden_ref.shape
    cuts, lanes = back_ref.shape[1:]

    def add(t, carry):
        acc = jnp.zeros((cuts, lanes), f32)
        for k in range(topk):
            acc = acc + weight_ref[t, k] * back_ref[slot_ref[t * topk + k]].astype(f32)
        total[pl.ds(pl.multiple_of(t * cuts, cuts), cuts), :] = acc
        return carry

    lax.fori_loop(0, tokens, add, 0, unroll=4)
    for j in range(cuts):
        span = slice(j * lanes, (j + 1) * lanes)
        mixture = total[pl.ds(j, tokens, stride=cuts), :]
        out_ref[:, span] = (hidden_ref[:, span] + mixture).astype(bf16)


def shards(
    query_proj,
    key_proj,
    value_proj,
    output_gate,
    beta_logit,
    log_decay,
    norm_gain,
    out_weight,
    residual,
    moe_gain,
    expert_ids,
    route_weight,
    expert_gate,
    expert_up,
    expert_down,
):
    length, dk = query_proj.shape
    heads = beta_logit.shape[0]
    tokens, width = residual.shape
    experts_here, _, hidden_units = expert_gate.shape
    groups = lax.axis_size("ctx")
    topk = expert_ids.shape[1]
    capacity = 6
    lanes = 128
    cuts = width // lanes
    slots = groups * experts_here * capacity
    columns = 4
    pairs = lax.axis_size("exp") // 2
    rows = groups // columns
    along_x = [[y * columns + i for i in range(columns)] for y in range(rows)]
    along_y = [[y * columns + i for y in range(rows)] for i in range(columns)]
    half = dk * heads // columns

    def pair_swap(block):
        return lax.ppermute(block, "exp", [(i, i ^ 1) for i in range(2 * pairs)])

    def exchange(blocks, groups):
        return lax.all_to_all(blocks, "ctx", 0, 0, tiled=True, axis_index_groups=groups)

    other_weight = pair_swap(out_weight)

    slot, owner = pl.pallas_call(
        functools.partial(route_kernel, topk, capacity),
        out_shape=(
            jax.ShapeDtypeStruct((tokens * topk,), jnp.int32),
            jax.ShapeDtypeStruct((slots,), jnp.int32),
        ),
        in_specs=[smem()],
        out_specs=(smem(), smem()),
        scratch_shapes=[pltpu.SMEM((groups * experts_here,), jnp.int32)],
        name="route",
    )(expert_ids)

    early_halves = 7
    package = jax.ShapeDtypeStruct((3, pairs, tokens, heads * dk), bf16)
    carry, kept, sent, early, late = pl.pallas_call(
        functools.partial(scan_kernel, heads),
        out_shape=(
            jax.ShapeDtypeStruct((columns, heads, 2 * dk, dk), bf16),
            package,
            package,
            jax.ShapeDtypeStruct((early_halves, lanes // 2, hidden_units), bf16),
            jax.ShapeDtypeStruct((6 * experts_here - early_halves, lanes // 2, hidden_units), bf16),
        ),
        in_specs=[vmem()] * 6 + [anywhere()] * 3,
        out_specs=(vmem(),) * 5,
        scratch_shapes=[
            pltpu.SemaphoreType.DMA((2 * experts_here * (2 + hidden_units // lanes),))
        ],
        compiler_params=params(60),
        cost_estimate=cost(2e9, 4e6),
        name="scan",
    )(
        query_proj, key_proj, value_proj, beta_logit, log_decay, output_gate,
        expert_gate, expert_up, expert_down,
    )
    got = pair_swap(sent)
    early = lax.all_gather(early, "exp", axis=0)

    maps = exchange(carry, along_x)
    totals, before = pl.pallas_call(
        row_kernel,
        out_shape=(
            jax.ShapeDtypeStruct((rows, dk + half, dk), bf16),
            jax.ShapeDtypeStruct((heads, 2 * dk, dk), bf16),
        ),
        in_specs=[vmem()],
        out_specs=(vmem(), vmem()),
        compiler_params=params(16),
        cost_estimate=cost(5e7, 1e6),
        name="row",
    )(maps)
    other_before = pair_swap(before)
    totals = exchange(totals, along_y)
    quarter = pl.pallas_call(
        column_kernel,
        out_shape=jax.ShapeDtypeStruct((2 * columns, half, dk), bf16),
        in_specs=[vmem()],
        out_specs=vmem(),
        compiler_params=params(16),
        cost_estimate=cost(2e7, 5e5),
        name="column",
    )(totals)
    quarters = lax.all_to_all(
        quarter,
        ("ctx", "exp"),
        0,
        0,
        tiled=True,
        axis_index_groups=[
            [(y * columns + x) * 2 * pairs + 2 * z + c for c in range(2) for x in range(columns)]
            for y in range(rows)
            for z in range(pairs)
        ],
    )

    partial_sums = pl.pallas_call(
        project_kernel,
        out_shape=jax.ShapeDtypeStruct((pairs, tokens, width), bf16),
        in_specs=[vmem()] * 8,
        out_specs=vmem(),
        compiler_params=params(24),
        cost_estimate=cost(6e8, 4e6),
        name="project",
    )(
        quarters, before, other_before, kept, got, norm_gain.reshape(1, dk),
        out_weight, other_weight,
    )
    same_core = [[c + 2 * z for z in range(pairs)] for c in range(2)]
    parts = lax.all_to_all(
        partial_sums, "exp", 0, 0, tiled=True, axis_index_groups=same_core
    )

    hidden, outgoing, late = pl.pallas_call(
        dispatch_kernel,
        out_shape=(
            jax.ShapeDtypeStruct((tokens, width), f32),
            jax.ShapeDtypeStruct((slots, cuts, lanes), bf16),
            jax.ShapeDtypeStruct(late.shape, bf16),
        ),
        in_specs=[smem(), vmem(), vmem(), vmem(), vmem(), anywhere()],
        out_specs=(vmem(), vmem(), anywhere()),
        input_output_aliases={5: 2},
        scratch_shapes=[
            pltpu.VMEM((tokens * cuts, lanes), f32),
            pltpu.VMEM((tokens, cuts, lanes), bf16),
        ],
        compiler_params=params(32),
        cost_estimate=cost(1e6, 3e6),
        name="dispatch",
    )(owner, parts, residual, moe_gain.reshape(1, width), early[0, 0, :16, :lanes], late)
    late = lax.all_gather(late, "exp", axis=0)
    outgoing = outgoing.reshape(groups, experts_here, capacity, cuts, lanes)
    incoming = lax.all_to_all(outgoing, "ctx", 0, 0, tiled=True)

    answers = pl.pallas_call(
        expert_kernel,
        out_shape=jax.ShapeDtypeStruct(incoming.shape, bf16),
        in_specs=[vmem(), anywhere(), anywhere()],
        out_specs=anywhere(),
        scratch_shapes=[
            pltpu.VMEM((2 * pairs, 6 * experts_here, lanes // 2, hidden_units), bf16),
            pltpu.VMEM((experts_here, groups, capacity, cuts, lanes), bf16),
            pltpu.SemaphoreType.DMA((6 * experts_here,)),
            pltpu.SemaphoreType.DMA((experts_here,)),
        ]
        + [pltpu.VMEM((groups * capacity * cuts, lanes), f32)] * (2 * experts_here)
        + [pltpu.VMEM((groups * capacity, width), bf16)] * experts_here,
        compiler_params=params(48),
        cost_estimate=cost(3e9, 16e6),
        name="experts",
    )(incoming, early, late)
    returned = lax.all_to_all(answers, "ctx", 0, 0, tiled=True).reshape(slots, cuts, lanes)

    return pl.pallas_call(
        functools.partial(combine_kernel, topk),
        out_shape=jax.ShapeDtypeStruct((tokens, width), bf16),
        in_specs=[smem(), smem(), vmem(), vmem()],
        out_specs=vmem(),
        scratch_shapes=[pltpu.VMEM((tokens * cuts, lanes), f32)],
        compiler_params=params(32),
        cost_estimate=cost(1e6, 3e6),
        name="combine",
    )(slot, route_weight, returned, hidden)


def solution(mesh):
    placed = (
        P("ctx", "exp"),
        P("ctx", "exp"),
        P("ctx", "exp"),
        P("ctx", "exp"),
        P("exp", "ctx"),
        P("exp", "ctx"),
        P(),
        P("exp", None),
        P(("ctx", "exp"), None),
        P(),
        P(("ctx", "exp"), None),
        P(("ctx", "exp"), None),
        P("ctx", "exp", None),
        P("ctx", "exp", None),
        P("ctx", None, "exp"),
    )
    return jax.shard_map(
        shards, mesh=mesh, in_specs=placed, out_specs=P(("ctx", "exp"), None), check_vma=False
    )
```
